256 devices in a mesh: tile: 128 (over x_hi, y, z, core), member: 2 (over x_lo).
Axes of the slice: x: 4 (x_hi: 2, x_lo: 2; x = x_hi * 2 + x_lo), y: 4, z: 8, core: 2. Of those that a mesh axis runs over, the one named last changes fastest.
Arguments:
- states: bfloat16 [2, 128, 32, 32, 128], P('member', 'tile'), may hold values from -6 to 6
- cotangent: bfloat16 [2, 128, 32, 32, 128], P('member', 'tile'), may hold values from -6 to 6
- seam_codes: int32 [128, 4], replicated, may hold values from 0 to 7
- corner_codes: int32 [128, 4], replicated, may hold values from 0 to 4
- dw_kernel: float32 [2, 7, 7, 128], replicated, may hold values from -0.875 to 0.875
- dw_bias: float32 [2, 128], replicated, may hold values from -3 to 3
- norm_gain: float32 [2, 128], replicated, may hold values from 0.5 to 1.5
- norm_bias: float32 [2, 128], replicated, may hold values from -3 to 3
- up_weight: bfloat16 [2, 128, 512], replicated, may hold values from -0.5 to 0.5
- up_bias: float32 [2, 512], replicated, may hold values from -3 to 3
- down_weight: bfloat16 [2, 512, 128], replicated, may hold values from -0.25 to 0.25
- down_bias: float32 [2, 128], replicated, may hold values from -3 to 3
- layer_scale: float32 [2, 128], replicated, may hold values from 0.3 to 1
Outputs:
- out_states: bfloat16 [2, 128, 32, 32, 128], P('member', 'tile')
- input_grad: bfloat16 [2, 128, 32, 32, 128], P('member', 'tile')
- kernel_grad: float32 [2, 7, 7, 128], replicated
- conv_bias_grad: float32 [2, 128], replicated
- gain_grad: float32 [2, 128], replicated
- offset_grad: float32 [2, 128], replicated
- up_weight_grad: float32 [2, 128, 512], replicated
- up_bias_grad: float32 [2, 512], replicated
- down_weight_grad: float32 [2, 512, 128], replicated
- down_bias_grad: float32 [2, 128], replicated
- scale_grad: float32 [2, 128], replicated
The draws below stay inside these ranges and needn't reach their ends.
Inputs may be any that keep to these rules, and one draw needn't show every extreme that they name: Tile t takes the strip of its neighbour in edge direction d from the neighbour's edge seam_codes[t, d] mod 4 (0 north, 1 south, 2 west, 3 east), reversed along the edge when the code is 4 or more. `corner_codes`: codes 0 to 3 name the neighbour's corner block (north-west, north-east, south-west, south-east) that fills tile t's corner slot d; 4 marks a corner where three faces meet, filled with zeros.
All inputs are finite; a program needn't handle non-finite values.
Results may differ from the reference program's by a relative error of at most 0.008.
Values may be sent and summed in bfloat16 or wider, within the bound.
No kernel may reach another device: no remote copies, remote signals or barrier semaphores. Data moves between devices by JAX's collectives and lax.ppermute only.
A program may use at most 128 MiB of HBM per device.

```python
import math
import jax
import jax.numpy as jnp
from jax import lax

C = 128
HID = 512
S = 32
ROW = 4
BLOCKS = 2
TILES = 128
MEMBERS = 2


def draw_cotangent(key, part):
    key = jax.random.fold_in(key, 7)
    shape = (MEMBERS, TILES, S, S, C)
    ramp = jnp.power(3.0, jnp.arange(TILES, dtype=jnp.float32) / (TILES - 1))
    noise = jax.random.normal(key, shape, jnp.float32)
    values = 0.6 * noise * ramp[None, :, None, None, None]
    return jnp.clip(values, -6.0, 6.0).astype(jnp.bfloat16)


def set_ends(array, key, least, largest):
    index_at = [jax.random.randint(jax.random.fold_in(key, axis), (), 0, length) for axis, length in enumerate(array.shape)]
    widest = array.shape.index(max(array.shape))
    beside = index_at[:widest] + [(index_at[widest] + 1) % array.shape[widest]] + index_at[widest + 1:]
    return array.at[tuple(index_at)].set(least).at[tuple(beside)].set(largest)


def levels(key, extent, pieces, smallest, largest):
    loudness = 1.0
    for dim, parts in pieces:
        heights = jax.random.uniform(jax.random.fold_in(jax.random.fold_in(key, 6), dim), (parts,), jnp.float32, smallest / len(pieces), largest / len(pieces))
        loudness = loudness * jnp.repeat(jnp.exp(heights), extent[dim] // parts).reshape((-1,) + (1,) * (len(extent) - 1 - dim))
    return loudness


def gaussian(stream_key, dims, spread, reach, split=(), held_as=jnp.bfloat16):
    values = jax.random.normal(stream_key, dims, jnp.float32) * spread
    if len(split) > 0:
        values = levels(stream_key, dims, split, -0.22, 0.18) * values
    return jnp.clip(values, min=-reach, max=reach).astype(held_as)


def setup_inputs(seed: int = 0) -> dict:
    keys = jax.random.split(jax.random.key(seed), 14)
    return {
        "states": gaussian(keys[0], (MEMBERS, TILES, S, S, C), 1.0, 6.0, ((0, 2), (1, 128))),
        "cotangent": draw_cotangent(jax.random.fold_in(keys[13], 71), 0),
        "seam_codes": set_ends(jax.random.randint(keys[2], (TILES, 4), 0, 8), jax.random.fold_in(keys[2], 1), 0, 7).astype(jnp.int32),
        "corner_codes": set_ends(jax.random.randint(keys[3], (TILES, 4), 0, 5), jax.random.fold_in(keys[3], 1), 0, 4).astype(jnp.int32),
        "dw_kernel": gaussian(keys[4], (BLOCKS, 7, 7, C), 49 ** -0.5, 0.875, (), jnp.float32),
        "dw_bias": gaussian(keys[5], (BLOCKS, C), 0.5, 3.0, (), jnp.float32),
        "norm_gain": jnp.clip(1.0 + 0.1 * jax.random.normal(keys[6], (BLOCKS, C), jnp.float32), 0.5, 1.5),
        "norm_bias": gaussian(keys[7], (BLOCKS, C), 0.5, 3.0, (), jnp.float32),
        "up_weight": gaussian(keys[8], (BLOCKS, C, HID), C ** -0.5, 0.5),
        "up_bias": gaussian(keys[9], (BLOCKS, HID), 0.5, 3.0, (), jnp.float32),
        "down_weight": gaussian(keys[10], (BLOCKS, HID, C), HID ** -0.5, 0.25),
        "down_bias": gaussian(keys[11], (BLOCKS, C), 0.5, 3.0, (), jnp.float32),
        "layer_scale": jnp.clip(jnp.exp(jax.random.uniform(keys[12], (BLOCKS, C), jnp.float32, math.log(0.3), math.log(1.0))), 0.3, 1.0),
    }


EPSILON = 1e-06
GELU_C = 0.7978845608028654
GELU_A = 0.044715

def gelu_value(values):
    inner = GELU_C * (values + GELU_A * values * values * values)
    return 0.5 * values * (1.0 + jnp.tanh(inner))

def gelu_slope(values):
    inner = GELU_C * (values + GELU_A * values * values * values)
    tangent = jnp.tanh(inner)
    return 0.5 * (1.0 + tangent) + 0.5 * values * (1.0 - tangent * tangent) * GELU_C * (1.0 + 3.0 * GELU_A * values * values)

def edge_offsets():
    return (-ROW, ROW, -1, 1)

def corner_offsets():
    return (-ROW - 1, -ROW + 1, ROW - 1, ROW + 1)

def edge_strips(tile_field):
    north = tile_field[0:3]
    south = tile_field[-3:][::-1]
    west = jnp.transpose(tile_field[:, 0:3], (1, 0, 2))
    east = jnp.transpose(tile_field[:, -3:][:, ::-1], (1, 0, 2))
    return jnp.stack([north, south, west, east])

def corner_blocks(tile_field):
    return jnp.stack([tile_field[0:3, 0:3], tile_field[0:3, -3:], tile_field[-3:, 0:3], tile_field[-3:, -3:]])

def orient(strip_data, seam_code):
    return jnp.where(seam_code >= 4, strip_data[:, ::-1], strip_data)

def select_edge(edge_set, seam_code):
    chosen = lax.dynamic_index_in_dim(edge_set, (seam_code % 4).astype(jnp.int32), 0, keepdims=False)
    return orient(chosen, seam_code)

def select_corner(block_set, corner_code):
    chosen = lax.dynamic_index_in_dim(block_set, jnp.minimum(corner_code, 3).astype(jnp.int32), 0, keepdims=False)
    return jnp.where(corner_code < 4, chosen, jnp.zeros_like(chosen))

def assemble(tile_field, edges, corners):
    top = jnp.concatenate([corners[0], edges[0][::-1], corners[1]], axis=1)
    middle = jnp.concatenate([jnp.transpose(edges[2][::-1], (1, 0, 2)), tile_field, jnp.transpose(edges[3], (1, 0, 2))], axis=1)
    bottom = jnp.concatenate([corners[2], edges[1], corners[3]], axis=1)
    return jnp.concatenate([top, middle, bottom], axis=0)

def split_rims(grad_pad):
    north = grad_pad[0:3, 3:-3][::-1]
    south = grad_pad[-3:, 3:-3]
    west = jnp.transpose(grad_pad[3:-3, 0:3], (1, 0, 2))[::-1]
    east = jnp.transpose(grad_pad[3:-3, -3:], (1, 0, 2))
    corners = [grad_pad[0:3, 0:3], grad_pad[0:3, -3:], grad_pad[-3:, 0:3], grad_pad[-3:, -3:]]
    return ([north, south, west, east], corners, grad_pad[3:-3, 3:-3])

def embed_rims(interior, edge_sum, corner_sum):
    size = interior.shape[0]
    result = interior
    result = result.at[0:3].add(edge_sum[0])
    result = result.at[size - 3:].add(edge_sum[1][::-1])
    result = result.at[:, 0:3].add(jnp.transpose(edge_sum[2], (1, 0, 2)))
    result = result.at[:, size - 3:].add(jnp.transpose(edge_sum[3], (1, 0, 2))[:, ::-1])
    result = result.at[0:3, 0:3].add(corner_sum[0])
    result = result.at[0:3, size - 3:].add(corner_sum[1])
    result = result.at[size - 3:, 0:3].add(corner_sum[2])
    result = result.at[size - 3:, size - 3:].add(corner_sum[3])
    return result

def depthwise(padded, kernel, bias):
    size = padded.shape[0] - 6
    wide = padded.astype(jnp.float32)
    total = jnp.zeros((size, size, padded.shape[2]), jnp.float32) + bias
    for row_tap in range(7):
        for col_tap in range(7):
            total = total + wide[row_tap:row_tap + size, col_tap:col_tap + size] * kernel[row_tap, col_tap]
    return total

def contract_rows(left, right):
    return lax.dot_general(left, right, (((0,), (0,)), ((), ())), preferred_element_type=jnp.float32)

def contract_cols(left, right):
    return lax.dot_general(left, right, (((1,), (1,)), ((), ())), preferred_element_type=jnp.float32)

def block_forward(padded, params):
    kernel, conv_bias, gain, offset_bias, up_w, up_b, down_w, down_b, scale = params
    size = padded.shape[0] - 6
    width = padded.shape[2]
    conv = depthwise(padded, kernel, conv_bias).reshape(size * size, width)
    centred = conv - lax.optimization_barrier(jnp.mean(conv, axis=1, keepdims=True))
    inv_std = lax.rsqrt(lax.optimization_barrier(jnp.mean(centred * centred, axis=1, keepdims=True)) + EPSILON)
    standard = centred * inv_std
    normed = (standard * gain + offset_bias).astype(jnp.bfloat16)
    pre_act = jnp.dot(normed, up_w, preferred_element_type=jnp.float32) + up_b
    activated = gelu_value(pre_act).astype(jnp.bfloat16)
    branch = jnp.dot(activated, down_w, preferred_element_type=jnp.float32) + down_b
    residual_in = padded[3:-3, 3:-3].reshape(size * size, width).astype(jnp.float32)
    output = (residual_in + scale * branch).astype(jnp.bfloat16).reshape(size, size, width)
    return (output, (standard, inv_std, normed, pre_act, activated, branch))

def block_backward(padded, saved, upstream, params):
    kernel, conv_bias, gain, offset_bias, up_w, up_b, down_w, down_b, scale = params
    standard, inv_std, normed, pre_act, activated, branch = saved
    size = padded.shape[0] - 6
    width = padded.shape[2]
    scale_grad = lax.optimization_barrier(jnp.sum(upstream * branch, axis=0))
    scaled = upstream * scale
    down_b_grad = lax.optimization_barrier(jnp.sum(scaled, axis=0))
    scaled_b = scaled.astype(jnp.bfloat16)
    down_w_grad = contract_rows(activated, scaled_b)
    act_grad = contract_cols(scaled_b, down_w)
    pre_grad = act_grad * gelu_slope(pre_act)
    up_b_grad = lax.optimization_barrier(jnp.sum(pre_grad, axis=0))
    pre_grad_b = pre_grad.astype(jnp.bfloat16)
    up_w_grad = contract_rows(normed, pre_grad_b)
    normed_grad = contract_cols(pre_grad_b, up_w)
    gain_grad = lax.optimization_barrier(jnp.sum(normed_grad * standard, axis=0))
    offset_grad = lax.optimization_barrier(jnp.sum(normed_grad, axis=0))
    std_grad = normed_grad * gain
    conv_grad = inv_std * (std_grad - lax.optimization_barrier(jnp.mean(std_grad, axis=1, keepdims=True)) - standard * lax.optimization_barrier(jnp.mean(std_grad * standard, axis=1, keepdims=True)))
    conv_bias_grad = lax.optimization_barrier(jnp.sum(conv_grad, axis=0))
    conv_field = conv_grad.reshape(size, size, width)
    wide = padded.astype(jnp.float32)
    kernel_rows = []
    for row_tap in range(7):
        kernel_cols = []
        for col_tap in range(7):
            kernel_cols.append(lax.optimization_barrier(jnp.sum(wide[row_tap:row_tap + size, col_tap:col_tap + size] * conv_field, axis=(0, 1))))
        kernel_rows.append(jnp.stack(kernel_cols))
    kernel_grad = jnp.stack(kernel_rows)
    grown = jnp.pad(conv_field, ((6, 6), (6, 6), (0, 0)))
    pad_grad = jnp.zeros((size + 6, size + 6, width), jnp.float32)
    for row_tap in range(7):
        for col_tap in range(7):
            pad_grad = pad_grad + grown[6 - row_tap:12 - row_tap + size, 6 - col_tap:12 - col_tap + size] * kernel[row_tap, col_tap]
    grads = (kernel_grad, conv_bias_grad, gain_grad, offset_grad, up_w_grad, up_b_grad, down_w_grad, down_b_grad, scale_grad)
    return (pad_grad, grads)

def per_tile(function):
    return jax.vmap(jax.vmap(function), in_axes=(0, None))

def halo_all(current, seam_codes, corner_codes):
    edge_set = jax.vmap(jax.vmap(edge_strips))(current)
    block_set = jax.vmap(jax.vmap(corner_blocks))(current)
    edges = []
    corners = []
    for facing in range(4):
        moved = jnp.roll(edge_set, -edge_offsets()[facing], axis=1)
        edges.append(per_tile(select_edge)(moved, seam_codes[:, facing]))
    for facing in range(4):
        moved = jnp.roll(block_set, -corner_offsets()[facing], axis=1)
        corners.append(per_tile(select_corner)(moved, corner_codes[:, facing]))
    return jax.vmap(jax.vmap(assemble))(current, edges, corners)

def return_all(pad_grads, seam_codes, corner_codes):
    edges, corners, interior = jax.vmap(jax.vmap(split_rims))(pad_grads)
    members, tiles, size, width = (interior.shape[0], interior.shape[1], interior.shape[2], interior.shape[4])
    edge_sum = jnp.zeros((members, tiles, 4, 3, size, width), jnp.float32)
    corner_sum = jnp.zeros((members, tiles, 4, 3, 3, width), jnp.float32)
    slots = jnp.arange(4, dtype=jnp.int32)
    for facing in range(4):
        offset = edge_offsets()[facing]
        sent = per_tile(orient)(edges[facing], seam_codes[:, facing])
        arrived = jnp.roll(sent, offset, axis=1)
        source_code = jnp.roll(seam_codes[:, facing], offset)
        chosen = (slots[None, :] == (source_code % 4)[:, None]).astype(jnp.float32)
        edge_sum = edge_sum + chosen[None, :, :, None, None, None] * arrived[:, :, None]
    for facing in range(4):
        offset = corner_offsets()[facing]
        live = (corner_codes[:, facing] < 4)[None, :, None, None, None]
        sent = jnp.where(live, corners[facing], jnp.zeros_like(corners[facing]))
        arrived = jnp.roll(sent, offset, axis=1)
        source_code = jnp.roll(corner_codes[:, facing], offset)
        chosen = (slots[None, :] == source_code[:, None]).astype(jnp.float32)
        corner_sum = corner_sum + chosen[None, :, :, None, None, None] * arrived[:, :, None]
    return jax.vmap(jax.vmap(embed_rims))(interior, edge_sum, corner_sum)

def reference(states, cotangent, seam_codes, corner_codes, dw_kernel, dw_bias, norm_gain, norm_bias, up_weight, up_bias, down_weight, down_bias, layer_scale):
    members, tiles, size, width = (states.shape[0], states.shape[1], states.shape[2], states.shape[4])
    stacks = (dw_kernel, dw_bias, norm_gain, norm_bias, up_weight, up_bias, down_weight, down_bias, layer_scale)
    current = states
    paddeds = []
    for block in range(BLOCKS):
        params = tuple((item[block] for item in stacks))
        padded = halo_all(current, seam_codes, corner_codes)
        paddeds.append(padded)
        flat = padded.reshape((members * tiles,) + padded.shape[2:])
        outputs = lax.map(lambda item_pad: block_forward(item_pad, params)[0], flat)
        current = outputs.reshape(states.shape)
    upstream = cotangent.astype(jnp.float32)
    collected = [None] * BLOCKS
    for block in reversed(range(BLOCKS)):
        params = tuple((item[block] for item in stacks))
        flat = paddeds[block].reshape((members * tiles,) + paddeds[block].shape[2:])
        flat_up = upstream.reshape(members * tiles, size * size, width)

        def local_pass(items):
            item_pad, item_up = items
            saved = block_forward(item_pad, params)[1]
            return block_backward(item_pad, saved, item_up, params)
        pad_grads, grads = lax.map(local_pass, (flat, flat_up))
        collected[block] = tuple((lax.optimization_barrier(jnp.sum(item, axis=0)) for item in grads))
        pad_grads = pad_grads.reshape((members, tiles) + pad_grads.shape[1:])
        upstream = upstream + return_all(pad_grads, seam_codes, corner_codes)
    factor = 1.0 / math.sqrt(members * tiles * size * size)
    stacked = [jnp.stack([collected[block][kind] for block in range(BLOCKS)]) * factor for kind in range(9)]
    return (current, upstream.astype(jnp.bfloat16), stacked[0], stacked[1], stacked[2], stacked[3], stacked[4], stacked[5], stacked[6], stacked[7], stacked[8])
```

```python
import math

import jax
import jax.numpy as jnp
from jax import lax
from jax.experimental import pallas as pl
from jax.experimental.pallas import tpu as pltpu
from jax.sharding import Mesh, PartitionSpec as P

BF = jnp.bfloat16
F32 = jnp.float32
BLOCKS = 2
SIZE = 32
CELLS = SIZE * SIZE
WIDTH = 128
HID = 512
TAPS = 7
CHUNK = 256
PAD_ROWS = 38
PAD_COLS = 48
GROWN_COLS = 64
MESSAGE = 128
EPSILON = 1e-06
GELU_C = 0.7978845608028654
GELU_A = 0.044715
TILE_AXES = ("far", "y", "z", "core")
VMEM_LIMIT = 32 * 1024 * 1024


def kernel_params():
    return pltpu.CompilerParams(vmem_limit_bytes=VMEM_LIMIT)


def whole(count):
    return [pl.BlockSpec(memory_space=pltpu.VMEM)] * count


def onehot(condition):
    return jnp.where(condition, 1.0, 0.0).astype(BF)


def matmul(left, right, dims=((1,), (0,))):
    return lax.dot_general(left, right, (dims, ((), ())), preferred_element_type=F32)


def message_cells(seam_ref, corner_ref, here, facing, slot):
    step = (4, -4, 1, -1)[facing]
    tiles = seam_ref.shape[0]
    code = seam_ref[(here + step + tiles) % tiles, facing]
    along = slot & 31
    depth = slot >> 5
    depth = 2 - depth if facing in (0, 2) else depth
    edge = code & 3
    along = jnp.where(code >= 4, 31 - along, along)
    depth = jnp.where((edge & 1) == 1, 31 - depth, depth)
    strip = jnp.where(edge < 2, depth * SIZE + along, along * SIZE + depth)
    if facing < 2:
        return jnp.where(slot < 96, strip, -1)
    if facing == 2:
        first, second = corner_ref[(here + 5) % tiles, 0], corner_ref[(here - 3 + tiles) % tiles, 2]
    else:
        first, second = corner_ref[(here - 5 + tiles) % tiles, 3], corner_ref[(here + 3) % tiles, 1]
    at = jnp.where(slot < 112, slot - 96, slot - 112)
    code = jnp.where(slot < 112, first, second)
    row = (at * 11) >> 5
    col = at - 3 * row
    block = (row + 29 * (code >> 1)) * SIZE + col + 29 * (code & 1)
    block = jnp.where((at < 9) & (code < 4), block, -1)
    return jnp.where(slot < 96, strip, block)


def select_kernel(here_ref, seam_ref, corner_ref, field_ref, sent_ref, gather_ref):
    here = here_ref[0]
    field = field_ref[...]
    slot = lax.broadcasted_iota(jnp.int32, (MESSAGE, WIDTH), 0)
    lane = lax.broadcasted_iota(jnp.int32, (MESSAGE, WIDTH), 1)
    for facing in range(4):
        cells = message_cells(seam_ref, corner_ref, here, facing, slot)
        total = jnp.zeros((MESSAGE, WIDTH), F32)
        for part in range(CELLS // WIDTH):
            chosen = onehot(cells == lane + part * WIDTH)
            gather_ref[facing * MESSAGE : (facing + 1) * MESSAGE, part * WIDTH : (part + 1) * WIDTH] = chosen
            total = total + matmul(chosen, field[part * WIDTH : (part + 1) * WIDTH])
        sent_ref[facing] = total.astype(BF)


def scatter_kernel(here_ref, seam_ref, corner_ref, scatter_ref):
    here = here_ref[0]
    slot = lax.broadcasted_iota(jnp.int32, (8, MESSAGE), 1)
    cell = lax.broadcasted_iota(jnp.int32, (CELLS, MESSAGE), 0)
    for facing in range(4):
        cells = message_cells(seam_ref, corner_ref, here, facing, slot)
        scatter_ref[:, facing * MESSAGE : (facing + 1) * MESSAGE] = onehot(cell == cells[0:1])


def row_rim_slots(position):
    depth = jnp.where(position >= 96, 2, jnp.where(position >= 48, 1, 0))
    along = position - 48 * depth - 5
    slot = jnp.where(
        along < 3, 96 + 3 * depth + along, jnp.where(along < 35, 32 * depth + along - 3, 77 + 3 * depth + along)
    )
    return jnp.where((along >= 0) & (along < 38), slot, -1)


def col_rim_slots(position, first):
    depth = (position & 7) - first
    slot = 32 * depth + (position >> 3)
    return jnp.where((depth >= 0) & (depth < 3), slot, -1)


def iota(shape, dim):
    return lax.broadcasted_iota(jnp.int32, shape, dim)


def fill_padded(padded_ref, field, north, south, west, east):
    rows = (3 * PAD_COLS, MESSAGE)
    place = onehot(row_rim_slots(iota(rows, 0)) == iota(rows, 1))
    padded_ref[0:3] = matmul(place, north).reshape(3, PAD_COLS, WIDTH)
    padded_ref[35:38] = matmul(place, south).reshape(3, PAD_COLS, WIDTH)
    cols = (SIZE * 8, MESSAGE)
    place = onehot(col_rim_slots(iota(cols, 0), 5) == iota(cols, 1))
    padded_ref[3:35, 0:8] = matmul(place, west).reshape(SIZE, 8, WIDTH)
    place = onehot(col_rim_slots(iota(cols, 0), 0) == iota(cols, 1))
    padded_ref[3:35, 40:48] = matmul(place, east).reshape(SIZE, 8, WIDTH)
    padded_ref[3:35, 8:40] = field.astype(F32).reshape(SIZE, SIZE, WIDTH)


def tap(kernel_ref, row_tap, col_tap):
    return kernel_ref[row_tap * TAPS + col_tap : row_tap * TAPS + col_tap + 1, :]


def convolve(source_ref, first_col, kernel_ref, flipped, start, out_ref):
    def group(index, carry):
        totals = [jnp.broadcast_to(start, (SIZE, WIDTH)) for _ in range(4)]
        for col_tap in range(TAPS):
            for row in range(4 + TAPS - 1):
                values = source_ref[index * 4 + row, first_col + col_tap : first_col + col_tap + SIZE, :]
                for out in range(max(0, row - TAPS + 1), min(4, row + 1)):
                    a, e = row - out, col_tap
                    if flipped:
                        a, e = TAPS - 1 - a, TAPS - 1 - e
                    totals[out] = totals[out] + values * tap(kernel_ref, a, e)
        for out in range(4):
            out_ref[pl.ds(pl.multiple_of(index * 128 + out * SIZE, SIZE), SIZE), :] = totals[out]
        return carry

    lax.fori_loop(0, SIZE // 4, group, 0)


def kernel_sums(padded_ref, grown_ref, sums_ref):
    sums_ref[...] = jnp.zeros_like(sums_ref)

    def group(index, carry):
        grads = [grown_ref[index * 4 + 3 + row, 16:48, :] for row in range(4)]
        for col_tap in range(TAPS):
            totals = [jnp.zeros((8, WIDTH), F32) for _ in range(TAPS)]
            for row in range(4 + TAPS - 1):
                values = padded_ref[index * 4 + row, 5 + col_tap : 5 + col_tap + SIZE, :]
                for out in range(max(0, row - TAPS + 1), min(4, row + 1)):
                    product = values * grads[out]
                    totals[row - out] = totals[row - out] + (
                        (product[0:8] + product[8:16]) + (product[16:24] + product[24:32])
                    )
            for row_tap in range(TAPS):
                at = 8 * (row_tap * TAPS + col_tap)
                sums_ref[at : at + 8, :] += totals[row_tap]
        return carry

    lax.fori_loop(0, SIZE // 4, group, 0)


def row_rim(grown_ref, kernel_ref, top):
    rows = []
    for depth in range(3):
        total = jnp.zeros((PAD_COLS, WIDTH), F32)
        for row_tap in range(TAPS):
            source = depth - row_tap if top else 35 + depth - row_tap
            if 0 <= source < SIZE:
                for col_tap in range(TAPS):
                    at = 11 - col_tap
                    total = total + grown_ref[source + 3, at : at + PAD_COLS, :] * tap(kernel_ref, row_tap, col_tap)
        rows.append(total)
    return jnp.concatenate(rows, axis=0)


def col_rim(grown_ref, kernel_ref, left, out_ref):
    def group(index, carry):
        totals = [jnp.zeros((8, WIDTH), F32) for _ in range(8)]
        for col_tap in range(3) if left else range(4, TAPS):
            at = 11 - col_tap if left else 51 - col_tap
            for row in range(8 + TAPS - 1):
                values = grown_ref[index * 8 + row, at : at + 8, :]
                for out in range(max(0, row - TAPS + 1), min(8, row + 1)):
                    totals[out] = totals[out] + values * tap(kernel_ref, TAPS - 1 - (row - out), col_tap)
        for out in range(8):
            out_ref[pl.ds(pl.multiple_of(index * 64 + out * 8, 8), 8), :] = totals[out]
        return carry

    lax.fori_loop(0, SIZE // 8, group, 0)


def send_rims(grown_ref, kernel_ref, rim_ref, sent_ref):
    rows = (MESSAGE, 3 * PAD_COLS)
    place = onehot(row_rim_slots(iota(rows, 1)) == iota(rows, 0))
    for facing in range(2):
        sent_ref[facing] = matmul(place, row_rim(grown_ref, kernel_ref, facing == 0).astype(BF)).astype(BF)
    cols = (MESSAGE, SIZE * 8)
    for facing in range(2, 4):
        col_rim(grown_ref, kernel_ref, facing == 2, rim_ref)
        place = onehot(col_rim_slots(iota(cols, 1), 5 if facing == 2 else 0) == iota(cols, 0))
        sent_ref[facing] = matmul(place, rim_ref[...].astype(BF)).astype(BF)


def normalised(conv):
    centred = conv - jnp.mean(conv, axis=1, keepdims=True)
    inv_std = lax.rsqrt(jnp.mean(centred * centred, axis=1, keepdims=True) + EPSILON)
    return centred * inv_std, inv_std


def forward_chunk(conv, field, rows, up_w, up_b, down_w):
    gain, offset, down_b, scale = rows
    standard, _ = normalised(conv)
    normed = (standard * gain + offset).astype(BF)
    pre = matmul(normed, up_w) + up_b
    tangent = jnp.tanh(pre * (GELU_C + (GELU_C * GELU_A) * pre * pre))
    activated = (0.5 * pre * (1.0 + tangent)).astype(BF)
    branch = matmul(activated, down_w) + down_b
    return (field.astype(F32) + scale * branch).astype(BF)


def first_kernel(
    field_ref, north_ref, south_ref, west_ref, east_ref, gather_ref, kernel_ref, bias_ref, gain_ref, offset_ref,
    up_ref, up_b_ref, down_ref, down_b_ref, scale_ref,
    out_ref, conv_ref, padded_ref, sent_ref,
):
    fill_padded(padded_ref, field_ref[...], north_ref[...], south_ref[...], west_ref[...], east_ref[...])
    convolve(padded_ref, 5, kernel_ref.at[0], False, bias_ref[0:1, :], conv_ref)
    rows = (gain_ref[0:1, :], offset_ref[0:1, :], down_b_ref[0:1, :], scale_ref[0:1, :])

    def chunk(index, carry):
        here = pl.ds(pl.multiple_of(index * CHUNK, CHUNK), CHUNK)
        out_ref[here, :] = forward_chunk(
            conv_ref[here, :], field_ref[here, :], rows, up_ref[0], up_b_ref[0:1, :], down_ref[0]
        )
        return carry

    lax.fori_loop(0, CELLS // CHUNK, chunk, 0)
    sent = matmul(gather_ref[...], out_ref[...]).astype(BF)
    for facing in range(4):
        sent_ref[facing] = sent[facing * MESSAGE : (facing + 1) * MESSAGE]


def backward_chunk(block, here, conv, upstream, refs, field, out_ref):
    (gain_ref, offset_ref, up_ref, up_b_ref, down_ref, down_b_ref, scale_ref, up_sum, down_sum, vector_sum, up_b_sum) = refs
    at = slice(block, block + 1)
    gain, scale = gain_ref[at, :], scale_ref[at, :]
    standard, inv_std = normalised(conv)
    normed = (standard * gain + offset_ref[at, :]).astype(BF)
    pre = matmul(normed, up_ref[block]) + up_b_ref[at, :]
    square = pre * pre
    tangent = jnp.tanh(pre * (GELU_C + (GELU_C * GELU_A) * square))
    half = 0.5 + 0.5 * tangent
    activated = (pre * half).astype(BF)
    slope = half + pre * (0.5 - 0.5 * tangent * tangent) * (GELU_C + (3.0 * GELU_C * GELU_A) * square)
    branch = matmul(activated, down_ref[block]) + down_b_ref[at, :]
    if out_ref is not None:
        out_ref[here, :] = (field.astype(F32) + scale * branch).astype(BF)
    scaled = upstream * scale
    scaled_b = scaled.astype(BF)
    down_sum[...] += matmul(scaled_b, activated, ((0,), (0,)))
    pre_grad = matmul(scaled_b, down_ref[block], ((1,), (1,))) * slope
    up_b_sum[...] += jnp.sum(pre_grad, axis=0, keepdims=True)
    pre_grad_b = pre_grad.astype(BF)
    up_sum[...] += matmul(normed, pre_grad_b, ((0,), (0,)))
    normed_grad = matmul(pre_grad_b, up_ref[block], ((1,), (1,)))
    std_grad = normed_grad * gain
    conv_grad = inv_std * (
        std_grad
        - jnp.mean(std_grad, axis=1, keepdims=True)
        - standard * jnp.mean(std_grad * standard, axis=1, keepdims=True)
    )
    for row, values in enumerate((conv_grad, normed_grad * standard, normed_grad, scaled, upstream * branch)):
        vector_sum[row : row + 1, :] += jnp.sum(values, axis=0, keepdims=True)
    return conv_grad


def backward_block(block, conv_ref, upstream_of, refs, field_ref, out_ref, grown_ref):
    for ref in refs[7:]:
        ref[...] = jnp.zeros_like(ref)
    grown_ref[0:3] = jnp.zeros((3, GROWN_COLS, WIDTH), F32)
    grown_ref[35:38] = jnp.zeros((3, GROWN_COLS, WIDTH), F32)
    grown_ref[3:35, 0:16] = jnp.zeros((SIZE, 16, WIDTH), F32)
    grown_ref[3:35, 48:64] = jnp.zeros((SIZE, 16, WIDTH), F32)
    tall = CHUNK // SIZE

    def chunk(index, carry):
        here = pl.ds(pl.multiple_of(index * CHUNK, CHUNK), CHUNK)
        field = None if field_ref is None else field_ref[here, :]
        grad = backward_chunk(block, here, conv_ref[here, :], upstream_of(here), refs, field, out_ref)
        grown_ref[pl.ds(3 + index * tall, tall), 16:48, :] = grad.reshape(tall, SIZE, WIDTH)
        return carry

    lax.fori_loop(0, CELLS // CHUNK, chunk, 0)


def pack_sums(refs, weights_ref, vectors_ref):
    up_sum, down_sum, vector_sum, up_b_sum = refs[7:]
    for part in range(HID // WIDTH):
        lanes = slice(part * WIDTH, (part + 1) * WIDTH)
        weights_ref[part * WIDTH : (part + 1) * WIDTH, :] = up_sum[:, lanes].astype(BF)
        weights_ref[HID + part * WIDTH : HID + (part + 1) * WIDTH, :] = down_sum[:, lanes].astype(BF)
        vector_sum[8 + part : 9 + part, :] = up_b_sum[:, lanes]
    vectors_ref[...] = vector_sum[...].astype(BF)


def second_kernel(
    field_ref, north_ref, south_ref, west_ref, east_ref, cotangent_ref, kernel_ref, bias_ref, gain_ref, offset_ref,
    up_ref, up_b_ref, down_ref, down_b_ref, scale_ref,
    out_ref, padded_ref, grown_ref, sent_ref, weights_ref, vectors_ref,
    conv_ref, up_sum, down_sum, vector_sum, up_b_sum, rim_ref,
):
    fill_padded(padded_ref, field_ref[...], north_ref[...], south_ref[...], west_ref[...], east_ref[...])
    convolve(padded_ref, 5, kernel_ref.at[1], False, bias_ref[1:2, :], conv_ref)
    refs = (gain_ref, offset_ref, up_ref, up_b_ref, down_ref, down_b_ref, scale_ref, up_sum, down_sum, vector_sum, up_b_sum)
    backward_block(
        1, conv_ref, lambda here: cotangent_ref[here, :].astype(F32), refs, field_ref, out_ref, grown_ref
    )
    send_rims(grown_ref, kernel_ref.at[1], rim_ref, sent_ref)
    pack_sums(refs, weights_ref, vectors_ref)


def third_kernel(
    conv_ref, cotangent_ref, inner_ref, first_ref, second_ref, third_ref, fourth_ref, scatter_ref, kernel_ref, gain_ref,
    offset_ref, up_ref, up_b_ref, down_ref, down_b_ref, scale_ref,
    upstream_ref, grown_ref, sent_ref, weights_ref, vectors_ref,
    up_sum, down_sum, vector_sum, up_b_sum, rim_ref,
):
    returned = jnp.concatenate([first_ref[...], second_ref[...], third_ref[...], fourth_ref[...]], axis=0)
    upstream_ref[...] = cotangent_ref[...].astype(F32) + inner_ref[...] + matmul(scatter_ref[...], returned)
    refs = (gain_ref, offset_ref, up_ref, up_b_ref, down_ref, down_b_ref, scale_ref, up_sum, down_sum, vector_sum, up_b_sum)
    backward_block(0, conv_ref, lambda here: upstream_ref[here, :], refs, None, None, grown_ref)
    send_rims(grown_ref, kernel_ref.at[0], rim_ref, sent_ref)
    pack_sums(refs, weights_ref, vectors_ref)


def last_kernel(upstream_ref, inner_ref, first_ref, second_ref, third_ref, fourth_ref, scatter_ref, out_ref):
    returned = jnp.concatenate([first_ref[...], second_ref[...], third_ref[...], fourth_ref[...]], axis=0)
    out_ref[...] = (upstream_ref[...] + inner_ref[...] + matmul(scatter_ref[...], returned)).astype(BF)


def make_inner_kernel(block):
    def inner_kernel(grown_ref, kernel_ref, inner_ref):
        convolve(grown_ref, 13, kernel_ref.at[block], True, jnp.zeros((1, WIDTH), F32), inner_ref)

    return inner_kernel


def taps_kernel(padded_ref, grown_ref, taps_ref, sums_ref):
    kernel_sums(padded_ref, grown_ref, sums_ref)
    taps_ref[...] = jnp.sum(sums_ref[...].reshape(64, 8, WIDTH), axis=1).astype(BF)


def passed_along(value, steps):
    count = lax.axis_size(TILE_AXES)
    return lax.ppermute(value, TILE_AXES, [(source, (source + steps) % count) for source in range(count)])


def give_halo(sent):
    west = passed_along(sent[2], 1)
    east = passed_along(sent[3], -1)
    north = passed_along(jnp.concatenate([sent[0, :96], west[96:112], east[112:]]), 4)
    south = passed_along(jnp.concatenate([sent[1, :96], west[112:], east[96:112]]), -4)
    return north, south, west, east


def give_back(sent):
    first = passed_along(sent[0], -4)
    second = passed_along(sent[1], 4)
    third = passed_along(jnp.concatenate([sent[2, :96], first[96:112], second[96:112]]), -1)
    fourth = passed_along(jnp.concatenate([sent[3, :96], second[112:], first[112:]]), 1)
    return first, second, third, fourth


REDUCED_ROWS = 2304


def swapped(value, axis):
    return lax.ppermute(value, axis, [(0, 1), (1, 0)])


def halved(value, axis):
    mine = lax.axis_index(axis)
    parts = value.reshape(2, value.shape[0] // 2, WIDTH)
    kept = lax.dynamic_index_in_dim(parts, mine, 0, keepdims=False)
    given = lax.dynamic_index_in_dim(parts, 1 - mine, 0, keepdims=False)
    return (kept.astype(F32) + swapped(given, axis).astype(F32)).astype(BF)


def joined(value, axis):
    other = swapped(value, axis)
    return jnp.where(
        lax.axis_index(axis) == 0, jnp.concatenate([value, other]), jnp.concatenate([other, value])
    )


def summed_apart(value, axes):
    count = lax.axis_size(axes)
    parts = lax.all_to_all(value, axes, 0, 0, tiled=True).reshape(count, -1, WIDTH)
    return jnp.sum(parts.astype(F32), axis=0).astype(BF)


def gathered(value, axes):
    count = lax.axis_size(axes)
    copies = jnp.broadcast_to(value[None], (count,) + value.shape).reshape(-1, WIDTH)
    return lax.all_to_all(copies, axes, 0, 0, tiled=True)


def summed_everywhere(value):
    value = halved(value, "core")
    value = summed_apart(value, ("far", "y", "z"))
    value = (value.astype(F32) + swapped(value, "member").astype(F32)).astype(BF)
    value = gathered(value, ("far", "y", "z"))
    return joined(value, "core")


def make_unpack_kernel(factor):
    def unpack_kernel(sum_ref, taps, conv_b, gain, offset, up, up_b, down, down_b, scale):
        for block in range(BLOCKS):
            base = block * 2 * HID
            for part in range(HID // WIDTH):
                rows = slice(base + part * WIDTH, base + (part + 1) * WIDTH)
                up[block, :, part * WIDTH : (part + 1) * WIDTH] = sum_ref[rows, :].astype(F32) * factor
                rows = slice(base + HID + part * WIDTH, base + HID + (part + 1) * WIDTH)
                down[block, part * WIDTH : (part + 1) * WIDTH, :] = (sum_ref[rows, :].astype(F32) * factor).T
            base = 4 * HID + 16 * block
            vectors = sum_ref[base : base + 16, :].astype(F32) * factor
            for row, ref in enumerate((conv_b, gain, offset, down_b, scale)):
                ref[block : block + 1, :] = vectors[row : row + 1]
            for part in range(HID // WIDTH):
                up_b[block : block + 1, part * WIDTH : (part + 1) * WIDTH] = vectors[8 + part : 9 + part]
            base = 4 * HID + 32 + 64 * block
            kernel_sum = sum_ref[base : base + 64, :].astype(F32) * factor
            for row_tap in range(TAPS):
                taps[block, row_tap] = kernel_sum[row_tap * TAPS : (row_tap + 1) * TAPS]

    return unpack_kernel


def shaped(*shapes):
    return [jax.ShapeDtypeStruct(shape, dtype) for shape, dtype in shapes]


def call(kernel, shapes, inputs, scratch=(), scalars=0, cost=None):
    specs = [pl.BlockSpec(memory_space=pltpu.SMEM)] * scalars + whole(len(inputs) - scalars)
    return pl.pallas_call(
        kernel,
        out_shape=shaped(*shapes),
        in_specs=specs,
        out_specs=whole(len(shapes)),
        scratch_shapes=list(scratch),
        compiler_params=kernel_params(),
        cost_estimate=cost,
    )(*inputs)


def body(
    states, cotangent, seam_codes, corner_codes, dw_kernel, dw_bias, norm_gain, norm_bias, up_weight, up_bias,
    down_weight, down_bias, layer_scale,
):
    count = lax.axis_size(TILE_AXES) * lax.axis_size("member")
    here = lax.axis_index(TILE_AXES).astype(jnp.int32).reshape(1)
    field = states.reshape(CELLS, WIDTH)
    upstream = cotangent.reshape(CELLS, WIDTH)
    taps = dw_kernel.reshape(BLOCKS, TAPS * TAPS, WIDTH)
    message = ((4, MESSAGE, WIDTH), BF)
    padded_shape = ((PAD_ROWS, PAD_COLS, WIDTH), F32)
    grown_shape = ((PAD_ROWS, GROWN_COLS, WIDTH), F32)
    cells = (CELLS, WIDTH)
    sums = [
        pltpu.VMEM((WIDTH, HID), F32),
        pltpu.VMEM((WIDTH, HID), F32),
        pltpu.VMEM((16, WIDTH), F32),
        pltpu.VMEM((1, HID), F32),
        pltpu.VMEM((SIZE * 8, WIDTH), F32),
    ]
    vpu = pl.CostEstimate(flops=2 * 49 * CELLS * WIDTH, bytes_accessed=3 << 20, transcendentals=0)

    sent, gather = call(
        select_kernel, [message, ((4 * MESSAGE, CELLS), BF)], [here, seam_codes, corner_codes, field], scalars=3
    )
    halo = give_halo(sent)
    (scatter,) = call(
        scatter_kernel, [((CELLS, 4 * MESSAGE), BF)], [here, seam_codes, corner_codes], scalars=3
    )
    vectors = (norm_gain, norm_bias, up_weight, up_bias, down_weight, down_bias, layer_scale)
    middle, conv, padded_0, sent = call(
        first_kernel,
        [(cells, BF), (cells, F32), padded_shape, message],
        [field, *halo, gather, taps, dw_bias, *vectors],
    )
    halo = give_halo(sent)
    out, padded_1, grown_1, sent, weights_1, vectors_1 = call(
        second_kernel,
        [(cells, BF), padded_shape, grown_shape, message, ((2 * HID, WIDTH), BF), ((16, WIDTH), BF)],
        [middle, *halo, upstream, taps, dw_bias, *vectors],
        [pltpu.VMEM(cells, F32), *sums],
    )
    returned = give_back(sent)
    (inner_1,) = call(make_inner_kernel(1), [(cells, F32)], [grown_1, taps], cost=vpu)
    tap_scratch = [pltpu.VMEM((64 * 8, WIDTH), F32)]
    (taps_1,) = call(taps_kernel, [((64, WIDTH), BF)], [padded_1, grown_1], tap_scratch, cost=vpu)
    upstream_0, grown_0, sent, weights_0, vectors_0 = call(
        third_kernel,
        [(cells, F32), grown_shape, message, ((2 * HID, WIDTH), BF), ((16, WIDTH), BF)],
        [conv, upstream, inner_1, *returned, scatter, taps, *vectors],
        sums,
    )
    returned = give_back(sent)
    (inner_0,) = call(make_inner_kernel(0), [(cells, F32)], [grown_0, taps], cost=vpu)
    (taps_0,) = call(taps_kernel, [((64, WIDTH), BF)], [padded_0, grown_0], tap_scratch, cost=vpu)
    (grad_field,) = call(last_kernel, [(cells, BF)], [upstream_0, inner_0, *returned, scatter])
    blank = jnp.zeros((REDUCED_ROWS - 4 * HID - 160, WIDTH), BF)
    total = summed_everywhere(
        jnp.concatenate([weights_0, weights_1, vectors_0, vectors_1, taps_0, taps_1, blank])
    )
    row, wide = ((BLOCKS, WIDTH), F32), ((BLOCKS, HID), F32)
    grads = call(
        make_unpack_kernel(1.0 / math.sqrt(count * CELLS)),
        [
            ((BLOCKS, TAPS, TAPS, WIDTH), F32), row, row, row, ((BLOCKS, WIDTH, HID), F32), wide,
            ((BLOCKS, HID, WIDTH), F32), row, row,
        ],
        [total],
    )
    shape = states.shape
    return (out.reshape(shape), grad_field.reshape(shape), *grads)


def solution(mesh):
    split = Mesh(mesh.devices.reshape(2, 4, 8, 2, 2), (*TILE_AXES, "member"))
    field = P("member", TILE_AXES, None, None, None)
    return jax.shard_map(
        body,
        mesh=split,
        in_specs=(field, field) + (P(),) * 11,
        out_specs=(field, field) + (P(),) * 9,
        check_vma=False,
    )
```

```python
import math

import jax
import jax.numpy as jnp
from jax import lax
from jax.experimental import pallas as pl
from jax.experimental.pallas import tpu as pltpu
from jax.sharding import Mesh, PartitionSpec as P

BF = jnp.bfloat16
F32 = jnp.float32
BLOCKS = 2
SIZE = 32
CELLS = SIZE * SIZE
WIDTH = 128
HID = 512
TAPS = 7
CHUNK = 256
PAD_ROWS = 38
PAD_COLS = 48
GROWN_COLS = 64
MESSAGE = 128
TILES = 128
PARAM_ROWS = 58
EPSILON = 1e-06
GELU_C = 0.7978845608028654
GELU_A = 0.044715
TILE_AXES = ("far", "y", "z", "core")
VMEM_LIMIT = 16 * 1024 * 1024


def kernel_params():
    return pltpu.CompilerParams(vmem_limit_bytes=VMEM_LIMIT)


def whole(count):
    return [pl.BlockSpec(memory_space=pltpu.VMEM)] * count


def onehot(condition):
    return jnp.where(condition, 1.0, 0.0).astype(BF)


def matmul(left, right, dims=((1,), (0,))):
    return lax.dot_general(left, right, (dims, ((), ())), preferred_element_type=F32)


def strip_cells(code, slot, facing):
    along = slot & 31
    depth = slot >> 5
    depth = 2 - depth if facing in (0, 2) else depth
    edge = code & 3
    along = jnp.where(code >= 4, 31 - along, along)
    depth = jnp.where((edge & 1) == 1, 31 - depth, depth)
    return jnp.where(edge < 2, depth * SIZE + along, along * SIZE + depth)


def corner_cells(first, second, slot):
    at = jnp.where(slot < 112, slot - 96, slot - 112)
    code = jnp.where(slot < 112, first, second)
    row = (at * 11) >> 5
    col = at - 3 * row
    block = (row + 29 * (code >> 1)) * SIZE + col + 29 * (code & 1)
    return jnp.where((at >= 0) & (at < 9) & (code < 4), block, -1)


def side_of(here, shift):
    return (here >> shift) & 1


def slot_of_facing(here, facing):
    row_side, col_side = side_of(here, 2), side_of(here, 0)
    return (row_side, 1 - row_side, 2 + col_side, 3 - col_side)[facing]


def seam_of(codes_ref, here, facing):
    step = (4, -4, 1, -1)[facing]
    return codes_ref[facing, (here + step) & (TILES - 1)]


def corner_of(codes_ref, here, step, direction):
    return codes_ref[4 + direction, (here + step) & (TILES - 1)]


def gathered_cells(codes_ref, here, facing, slot):
    strip = strip_cells(seam_of(codes_ref, here, facing), slot, facing)
    if facing < 2:
        return jnp.where(slot < 96, strip, -1)
    if facing == 2:
        below, above = corner_of(codes_ref, here, 5, 0), corner_of(codes_ref, here, -3, 2)
        flip = side_of(here + 1, 2)
    else:
        below, above = corner_of(codes_ref, here, 3, 1), corner_of(codes_ref, here, -5, 3)
        flip = side_of(here - 1, 2)
    first, second = jnp.where(flip == 0, below, above), jnp.where(flip == 0, above, below)
    return jnp.where(slot < 96, strip, corner_cells(first, second, slot))


def scattered_cells(codes_ref, here, facing, slot):
    strip = strip_cells(seam_of(codes_ref, here, facing), slot, facing)
    if facing >= 2:
        return jnp.where(slot < 96, strip, -1)
    if facing == 0:
        right, left = corner_of(codes_ref, here, 5, 0), corner_of(codes_ref, here, 3, 1)
    else:
        right, left = corner_of(codes_ref, here, -3, 2), corner_of(codes_ref, here, -5, 3)
    flip = side_of(here, 0)
    first, second = jnp.where(flip == 0, right, left), jnp.where(flip == 0, left, right)
    return jnp.where(slot < 96, strip, corner_cells(first, second, slot))


def select_kernel(here_ref, codes_ref, field_ref, sent_ref, gather_ref, owners_ref):
    here = here_ref[0]
    slot = iota((MESSAGE, WIDTH), 0)
    lane = iota((MESSAGE, WIDTH), 1)
    for facing in range(4):
        cells = gathered_cells(codes_ref, here, facing, slot)
        for part in range(CELLS // WIDTH):
            chosen = onehot(cells == lane + part * WIDTH)
            gather_ref[facing * MESSAGE : (facing + 1) * MESSAGE, part * WIDTH : (part + 1) * WIDTH] = chosen
    send_cells(here, gather_ref[...], field_ref[...], sent_ref)
    slot = iota((8, MESSAGE), 1)
    for facing in range(4):
        owners_ref[slot_of_facing(here, facing)] = scattered_cells(codes_ref, here, facing, slot)


def send_cells(here, gather, field, sent_ref):
    sent = matmul(gather, field).astype(BF)
    for facing in range(4):
        sent_ref[slot_of_facing(here, facing)] = sent[facing * MESSAGE : (facing + 1) * MESSAGE]


def scatter_kernel(owners_ref, scatter_ref):
    cell = iota((CELLS, MESSAGE), 0)
    for slot in range(4):
        scatter_ref[:, slot * MESSAGE : (slot + 1) * MESSAGE] = onehot(cell == owners_ref[slot][0:1])


def row_rim_slots(position, strip, left=None, right=None):
    depth = jnp.where(position >= 96, 2, jnp.where(position >= 48, 1, 0))
    along = position - 48 * depth - 5
    slot = jnp.full_like(position, -1)
    if strip:
        slot = jnp.where((along >= 3) & (along < 35), 32 * depth + along - 3, slot)
    if left is not None:
        slot = jnp.where((along >= 0) & (along < 3), left + 3 * depth + along, slot)
    if right is not None:
        slot = jnp.where((along >= 35) & (along < 38), right + 3 * depth + along - 35, slot)
    return slot


def col_rim_slots(position, first):
    depth = (position & 7) - first
    slot = 32 * depth + (position >> 3)
    return jnp.where((depth >= 0) & (depth < 3), slot, -1)


def iota(shape, dim):
    return lax.broadcasted_iota(jnp.int32, shape, dim)


def fill_inside(padded_ref, here, field, by_a, by_b):
    side = side_of(here, 0)
    west, east = jnp.where(side == 0, by_b, by_a), jnp.where(side == 0, by_a, by_b)
    cols = (SIZE * 8, MESSAGE)
    place = onehot(col_rim_slots(iota(cols, 0), 5) == iota(cols, 1))
    padded_ref[3:35, 0:8] = matmul(place, west).reshape(SIZE, 8, WIDTH)
    place = onehot(col_rim_slots(iota(cols, 0), 0) == iota(cols, 1))
    padded_ref[3:35, 40:48] = matmul(place, east).reshape(SIZE, 8, WIDTH)
    padded_ref[3:35, 8:40] = field.astype(F32).reshape(SIZE, SIZE, WIDTH)


def fill_rims(padded_ref, here, by_c, by_d):
    row_side, col_side = side_of(here, 2), side_of(here, 0)
    north, south = jnp.where(row_side == 0, by_d, by_c), jnp.where(row_side == 0, by_c, by_d)
    rows = (3 * PAD_COLS, MESSAGE)
    slots = row_rim_slots(iota(rows, 0), True, 112 - 16 * col_side, 96 + 16 * col_side)
    place = onehot(slots == iota(rows, 1))
    padded_ref[0:3] = matmul(place, north).reshape(3, PAD_COLS, WIDTH)
    padded_ref[35:38] = matmul(place, south).reshape(3, PAD_COLS, WIDTH)


def tap(kernel, row_tap, col_tap):
    ref, block = kernel
    return ref[row_tap * TAPS + col_tap, block : block + 1, :]


def convolve(source_ref, first_col, kernel_ref, flipped, start, out_ref, first=0, last=SIZE // 4):
    def group(index, carry):
        totals = [jnp.broadcast_to(start, (SIZE, WIDTH)) for _ in range(4)]
        for col_tap in range(TAPS):
            for row in range(4 + TAPS - 1):
                values = source_ref[index * 4 + row, first_col + col_tap : first_col + col_tap + SIZE, :]
                for out in range(max(0, row - TAPS + 1), min(4, row + 1)):
                    a, e = row - out, col_tap
                    if flipped:
                        a, e = TAPS - 1 - a, TAPS - 1 - e
                    totals[out] = totals[out] + values * tap(kernel_ref, a, e)
        for out in range(4):
            out_ref[pl.ds(pl.multiple_of(index * 128 + out * SIZE, SIZE), SIZE), :] = totals[out]
        return carry

    lax.fori_loop(first, last, group, 0)


def kernel_sums(padded_ref, grad_ref, sums_ref):
    sums_ref[...] = jnp.zeros_like(sums_ref)

    def group(index, carry):
        grads = [
            grad_ref[pl.ds(pl.multiple_of(index * 128 + row * SIZE, SIZE), SIZE), :] for row in range(4)
        ]
        for col_tap in range(TAPS):
            totals = [jnp.zeros((8, WIDTH), F32) for _ in range(TAPS)]
            for row in range(4 + TAPS - 1):
                values = padded_ref[index * 4 + row, 5 + col_tap : 5 + col_tap + SIZE, :]
                for out in range(max(0, row - TAPS + 1), min(4, row + 1)):
                    product = values * grads[out]
                    totals[row - out] = totals[row - out] + (
                        (product[0:8] + product[8:16]) + (product[16:24] + product[24:32])
                    )
            for row_tap in range(TAPS):
                at = 8 * (row_tap * TAPS + col_tap)
                sums_ref[at : at + 8, :] += totals[row_tap]
        return carry

    lax.fori_loop(0, SIZE // 4, group, 0)


def row_rim(grown_ref, kernel_ref, top):
    rows = []
    for depth in range(3):
        total = jnp.zeros((PAD_COLS, WIDTH), F32)
        for row_tap in range(TAPS):
            source = depth - row_tap if top else 35 + depth - row_tap
            if 0 <= source < SIZE:
                for col_tap in range(TAPS):
                    at = 11 - col_tap
                    total = total + grown_ref[source + 3, at : at + PAD_COLS, :] * tap(kernel_ref, row_tap, col_tap)
        rows.append(total)
    return jnp.concatenate(rows, axis=0)


def col_rim(grown_ref, kernel_ref, left, out_ref):
    def group(index, carry):
        totals = [jnp.zeros((8, WIDTH), F32) for _ in range(8)]
        for col_tap in range(3) if left else range(4, TAPS):
            at = 11 - col_tap if left else 51 - col_tap
            for row in range(8 + TAPS - 1):
                values = grown_ref[index * 8 + row, at : at + 8, :]
                for out in range(max(0, row - TAPS + 1), min(8, row + 1)):
                    totals[out] = totals[out] + values * tap(kernel_ref, TAPS - 1 - (row - out), col_tap)
        for out in range(8):
            out_ref[pl.ds(pl.multiple_of(index * 64 + out * 8, 8), 8), :] = totals[out]
        return carry

    lax.fori_loop(0, SIZE // 8, group, 0)


def send_rims(here, grown_ref, kernel, rim_ref, sent_ref):
    rows = (MESSAGE, 3 * PAD_COLS)
    place = onehot(row_rim_slots(iota(rows, 1), True) == iota(rows, 0))
    rims = []
    for facing in range(2):
        rim = row_rim(grown_ref, kernel, facing == 0).astype(BF)
        sent_ref[(1 - side_of(here, 2), side_of(here, 2))[facing]] = matmul(place, rim).astype(BF)
        rims.append(rim)
    cols = (MESSAGE, SIZE * 8)
    for left in (True, False):
        col_rim(grown_ref, kernel, left, rim_ref)
        place = onehot(col_rim_slots(iota(cols, 1), 5 if left else 0) == iota(cols, 0))
        message = matmul(place, rim_ref[...].astype(BF))
        flip = side_of(here - 1 if left else here + 1, 2)
        for rim, base in ((rims[0], 112 - 16 * flip), (rims[1], 96 + 16 * flip)):
            slots = row_rim_slots(iota(rows, 1), False, base if left else None, None if left else base)
            message = message + matmul(onehot(slots == iota(rows, 0)), rim)
        side = side_of(here, 0)
        sent_ref[3 - side if left else 2 + side] = message.astype(BF)


def normalised(conv):
    centred = conv - jnp.mean(conv, axis=1, keepdims=True)
    inv_std = lax.rsqrt(jnp.mean(centred * centred, axis=1, keepdims=True) + EPSILON)
    return centred * inv_std, inv_std


def forward_chunk(conv, field, rows, up_w, up_b, down_w):
    gain, offset, down_b, scale = rows
    standard, _ = normalised(conv)
    normed = (standard * gain + offset).astype(BF)
    pre = matmul(normed, up_w) + up_b
    tangent = jnp.tanh(pre * (GELU_C + (GELU_C * GELU_A) * pre * pre))
    activated = (0.5 * pre * (1.0 + tangent)).astype(BF)
    branch = matmul(activated, down_w) + down_b
    return (field.astype(F32) + scale * branch).astype(BF)


def block_rows(params_ref, block):
    rows = [params_ref[row, block : block + 1, :] for row in range(TAPS * TAPS, PARAM_ROWS)]
    return (*rows[:5], jnp.concatenate(rows[5:], axis=1))


EDGE = 4 * SIZE
INSIDE = CELLS - 2 * EDGE


def first_inside_kernel(
    here_ref, field_ref, a_ref, b_ref, params_ref, up_ref, down_ref,
    out_ref, conv_ref, padded_ref, full_ref,
):
    fill_inside(padded_ref, here_ref[0], field_ref[...], a_ref[...], b_ref[...])
    bias, gain, offset, down_b, scale, up_b = block_rows(params_ref, 0)
    convolve(padded_ref, 5, (params_ref, 0), False, bias, full_ref, 1, 7)

    def chunk(index, carry):
        at = pl.ds(pl.multiple_of(index * CHUNK, CHUNK), CHUNK)
        cells = pl.ds(pl.multiple_of(EDGE + index * CHUNK, EDGE), CHUNK)
        conv = full_ref[cells, :]
        conv_ref[at, :] = conv
        out_ref[at, :] = forward_chunk(
            conv, field_ref[cells, :], (gain, offset, down_b, scale), up_ref[0], up_b, down_ref[0]
        )
        return carry

    lax.fori_loop(0, INSIDE // CHUNK, chunk, 0)


def ends(ref):
    return jnp.concatenate([ref[:EDGE, :], ref[CELLS - EDGE :, :]], axis=0)


def join_rows(ref, inside, edges):
    ref[:EDGE, :] = edges[:EDGE]
    ref[EDGE : CELLS - EDGE, :] = inside
    ref[CELLS - EDGE :, :] = edges[EDGE:]


def first_kernel(
    here_ref, field_ref, c_ref, d_ref, a_ref, b_ref, out_in_ref, gather_ref, params_ref, up_ref, down_ref,
    out_ref, conv_ref, padded_ref, sent_ref, full_ref,
):
    here = here_ref[0]
    fill_inside(padded_ref, here, field_ref[...], a_ref[...], b_ref[...])
    fill_rims(padded_ref, here, c_ref[...], d_ref[...])
    bias, gain, offset, down_b, scale, up_b = block_rows(params_ref, 0)
    for index in (0, 7):
        convolve(padded_ref, 5, (params_ref, 0), False, bias, full_ref, index, index + 1)
    conv = ends(full_ref)
    conv_ref[...] = conv
    out = forward_chunk(conv, ends(field_ref), (gain, offset, down_b, scale), up_ref[0], up_b, down_ref[0])
    join_rows(out_ref, out_in_ref[...], out)
    send_cells(here, gather_ref[...], out_ref[...], sent_ref)


def again(block, conv, refs):
    params_ref, up_ref, down_ref = refs
    _, gain, offset, down_b, _, up_b = block_rows(params_ref, block)
    standard, inv_std = normalised(conv)
    normed = (standard * gain + offset).astype(BF)
    pre = matmul(normed, up_ref[block]) + up_b
    square = pre * pre
    tangent = jnp.tanh(pre * (GELU_C + (GELU_C * GELU_A) * square))
    half = 0.5 + 0.5 * tangent
    activated = (pre * half).astype(BF)
    slope = half + pre * (0.5 - 0.5 * tangent * tangent) * (GELU_C + (3.0 * GELU_C * GELU_A) * square)
    branch = matmul(activated, down_ref[block]) + down_b
    return standard, inv_std, normed, activated, slope, branch


def backward_chunk(block, saved, upstream, refs):
    params_ref, up_ref, down_ref, up_sum, down_sum, vector_sum, up_b_sum = refs
    standard, inv_std, normed, activated, slope, branch = saved
    _, gain, _, _, scale, _ = block_rows(params_ref, block)
    scaled = upstream * scale
    scaled_b = scaled.astype(BF)
    down_sum[...] += matmul(scaled_b, activated, ((0,), (0,)))
    pre_grad = matmul(scaled_b, down_ref[block], ((1,), (1,))) * slope
    up_b_sum[...] += jnp.sum(pre_grad, axis=0, keepdims=True)
    pre_grad_b = pre_grad.astype(BF)
    up_sum[...] += matmul(normed, pre_grad_b, ((0,), (0,)))
    normed_grad = matmul(pre_grad_b, up_ref[block], ((1,), (1,)))
    std_grad = normed_grad * gain
    conv_grad = inv_std * (
        std_grad
        - jnp.mean(std_grad, axis=1, keepdims=True)
        - standard * jnp.mean(std_grad * standard, axis=1, keepdims=True)
    )
    for row, values in enumerate((conv_grad, normed_grad * standard, normed_grad, scaled, upstream * branch)):
        vector_sum[row : row + 1, :] += jnp.sum(values, axis=0, keepdims=True)
    return conv_grad


def through(block, conv, upstream, field, refs):
    saved = again(block, conv, refs[:3])
    scale = block_rows(refs[0], block)[4]
    out = (field.astype(F32) + scale * saved[5]).astype(BF)
    return backward_chunk(block, saved, upstream, refs), out


def clear(refs):
    for ref in refs:
        ref[...] = jnp.zeros_like(ref)


def fill_grown(grown_ref, grad):
    grown_ref[0:3] = jnp.zeros((3, GROWN_COLS, WIDTH), F32)
    grown_ref[35:38] = jnp.zeros((3, GROWN_COLS, WIDTH), F32)
    grown_ref[3:35, 0:16] = jnp.zeros((SIZE, 16, WIDTH), F32)
    grown_ref[3:35, 48:64] = jnp.zeros((SIZE, 16, WIDTH), F32)
    grown_ref[3:35, 16:48] = grad.reshape(SIZE, SIZE, WIDTH)


def pack_sums(refs, weights_ref, vectors_ref):
    up_sum, down_sum, vector_sum, up_b_sum = refs[3:]
    for part in range(HID // WIDTH):
        lanes = slice(part * WIDTH, (part + 1) * WIDTH)
        weights_ref[part * WIDTH : (part + 1) * WIDTH, :] = up_sum[:, lanes].astype(BF)
        weights_ref[HID + part * WIDTH : HID + (part + 1) * WIDTH, :] = down_sum[:, lanes].astype(BF)
        vector_sum[8 + part : 9 + part, :] = up_b_sum[:, lanes]
    vectors_ref[...] = vector_sum[...].astype(BF)


def second_inside_kernel(
    here_ref, field_ref, a_ref, b_ref, cotangent_ref, params_ref, up_ref, down_ref,
    out_ref, grad_ref, up_sum, down_sum, vector_sum, up_b_sum, padded_ref, conv_ref,
):
    fill_inside(padded_ref, here_ref[0], field_ref[...], a_ref[...], b_ref[...])
    convolve(padded_ref, 5, (params_ref, 1), False, block_rows(params_ref, 1)[0], conv_ref, 1, 7)
    refs = (params_ref, up_ref, down_ref, up_sum, down_sum, vector_sum, up_b_sum)
    clear(refs[3:])

    def chunk(index, carry):
        at = pl.ds(pl.multiple_of(index * CHUNK, CHUNK), CHUNK)
        cells = pl.ds(pl.multiple_of(EDGE + index * CHUNK, EDGE), CHUNK)
        grad_ref[at, :], out_ref[at, :] = through(
            1, conv_ref[cells, :], cotangent_ref[cells, :].astype(F32), field_ref[cells, :], refs
        )
        return carry

    lax.fori_loop(0, INSIDE // CHUNK, chunk, 0)


def second_kernel(
    here_ref, field_ref, c_ref, d_ref, a_ref, b_ref, grad_in_ref, up_in, down_in, vector_in, up_b_in,
    cotangent_ref, params_ref, up_ref, down_ref,
    out_ref, padded_ref, grad_ref, sent_ref, weights_ref, sums_ref,
    conv_ref, grown_ref, up_sum, down_sum, vector_sum, up_b_sum, rim_ref,
):
    here = here_ref[0]
    fill_inside(padded_ref, here, field_ref[...], a_ref[...], b_ref[...])
    fill_rims(padded_ref, here, c_ref[...], d_ref[...])
    for index in (0, 7):
        convolve(padded_ref, 5, (params_ref, 1), False, block_rows(params_ref, 1)[0], conv_ref, index, index + 1)
    refs = (params_ref, up_ref, down_ref, up_sum, down_sum, vector_sum, up_b_sum)
    for ref, start in zip(refs[3:], (up_in, down_in, vector_in, up_b_in)):
        ref[...] = start[...]
    grad, out_ref[...] = through(1, ends(conv_ref), ends(cotangent_ref).astype(F32), ends(field_ref), refs)
    join_rows(grad_ref, grad_in_ref[...], grad)
    fill_grown(grown_ref, grad_ref[...])
    send_rims(here, grown_ref, (params_ref, 1), rim_ref, sent_ref)
    pack_sums(refs, weights_ref, sums_ref)


def third_again_kernel(
    conv_ref, conv_edge_ref, params_ref, up_ref, down_ref,
    standard_ref, inv_std_ref, normed_ref, activated_ref, slope_ref, branch_ref, full_ref,
):
    join_rows(full_ref, conv_ref[...], conv_edge_ref[...])

    def chunk(index, carry):
        at = pl.ds(pl.multiple_of(index * CHUNK, CHUNK), CHUNK)
        saved = again(0, full_ref[at, :], (params_ref, up_ref, down_ref))
        standard_ref[at, :], _, normed_ref[at, :], activated_ref[at, :], slope_ref[at, :], branch_ref[at, :] = saved
        inv_std_ref[at, :] = jnp.broadcast_to(saved[1], (CHUNK, WIDTH))
        return carry

    lax.fori_loop(0, CELLS // CHUNK, chunk, 0)


def third_kernel(
    here_ref, standard_ref, inv_std_ref, normed_ref, activated_ref, slope_ref, branch_ref, cotangent_ref, inner_ref,
    c_ref, d_ref, a_ref, b_ref, scatter_ref, params_ref, up_ref, down_ref,
    upstream_ref, grad_ref, sent_ref, weights_ref, sums_ref,
    grown_ref, up_sum, down_sum, vector_sum, up_b_sum, rim_ref,
):
    returned = jnp.concatenate([c_ref[...], d_ref[...], a_ref[...], b_ref[...]], axis=0)
    upstream_ref[...] = cotangent_ref[...].astype(F32) + inner_ref[...] + matmul(scatter_ref[...], returned)
    refs = (params_ref, up_ref, down_ref, up_sum, down_sum, vector_sum, up_b_sum)
    clear(refs[3:])
    saved_refs = (standard_ref, inv_std_ref, normed_ref, activated_ref, slope_ref, branch_ref)

    def chunk(index, carry):
        at = pl.ds(pl.multiple_of(index * CHUNK, CHUNK), CHUNK)
        grad_ref[at, :] = backward_chunk(0, [ref[at, :] for ref in saved_refs], upstream_ref[at, :], refs)
        return carry

    lax.fori_loop(0, CELLS // CHUNK, chunk, 0)
    fill_grown(grown_ref, grad_ref[...])
    send_rims(here_ref[0], grown_ref, (params_ref, 0), rim_ref, sent_ref)
    pack_sums(refs, weights_ref, sums_ref)


def last_kernel(upstream_ref, inner_ref, c_ref, d_ref, a_ref, b_ref, scatter_ref, out_ref):
    returned = jnp.concatenate([c_ref[...], d_ref[...], a_ref[...], b_ref[...]], axis=0)
    out_ref[...] = (upstream_ref[...] + inner_ref[...] + matmul(scatter_ref[...], returned)).astype(BF)


def make_inner_kernel(block):
    def inner_kernel(grad_ref, params_ref, inner_ref, grown_ref):
        fill_grown(grown_ref, grad_ref[...])
        convolve(grown_ref, 13, (params_ref, block), True, jnp.zeros((1, WIDTH), F32), inner_ref)

    return inner_kernel


def taps_and_out_kernel(padded_ref, grad_ref, inside_ref, edges_ref, taps_ref, out_ref, sums_ref):
    join_rows(out_ref, inside_ref[...], edges_ref[...])
    taps_kernel(padded_ref, grad_ref, taps_ref, sums_ref)


def taps_kernel(padded_ref, grad_ref, taps_ref, sums_ref):
    kernel_sums(padded_ref, grad_ref, sums_ref)
    taps_ref[...] = jnp.sum(sums_ref[...].reshape(64, 8, WIDTH), axis=1).astype(BF)


def halves_kernel(
    core_ref, padded_ref, grad_ref, weights_0_ref, sums_0_ref, weights_1_ref, sums_1_ref, taps_1_ref,
    kept_ref, given_ref, taps_ref, partial_ref,
):
    taps_kernel(padded_ref, grad_ref, taps_ref, partial_ref)

    def fill(half_ref, *parts):
        at = 0
        for part in parts:
            half_ref[at : at + part.shape[0], :] = part[...]
            at += part.shape[0]
        half_ref[at:, :] = jnp.zeros((HALF_ROWS - at, WIDTH), BF)

    first = (weights_0_ref, sums_0_ref, taps_ref)
    second = (weights_1_ref, sums_1_ref, taps_1_ref)
    for core, kept, given in ((0, first, second), (1, second, first)):

        @pl.when(core_ref[0] == core)
        def _(kept=kept, given=given):
            fill(kept_ref, *kept)
            fill(given_ref, *given)


def swapped_tiles(value, step, odd):
    starts = [tile for tile in range(TILES) if (tile // step) % 2 == odd]
    pairs = [(tile, (tile + step) % TILES) for tile in starts]
    return lax.ppermute(value, TILE_AXES, pairs + [(target, source) for source, target in pairs])


def beside(sent):
    return swapped_tiles(sent[2], 1, 0), swapped_tiles(sent[3], 1, 1)


def beyond(sent, by_a, by_b):
    by_c = swapped_tiles(jnp.concatenate([sent[0, :96], by_a[96:112], by_b[96:112]]), 4, 0)
    by_d = swapped_tiles(jnp.concatenate([sent[1, :96], by_a[112:], by_b[112:]]), 4, 1)
    return by_c, by_d


def after(values, *others):
    return lax.optimization_barrier((values, others))[0]


HALF_ROWS = 1152


def swapped(value, axis):
    return lax.ppermute(value, axis, [(0, 1), (1, 0)])


def joined(value, axis):
    other = swapped(value, axis)
    return jnp.where(
        lax.axis_index(axis) == 0, jnp.concatenate([value, other]), jnp.concatenate([other, value])
    )


def summed_apart(value, axes):
    count = lax.axis_size(axes)
    parts = lax.all_to_all(value, axes, 0, 0, tiled=True).reshape(count, -1, WIDTH)
    return jnp.sum(parts.astype(F32), axis=0).astype(BF)


def gathered(value, axes):
    count = lax.axis_size(axes)
    copies = jnp.broadcast_to(value[None], (count,) + value.shape).reshape(-1, WIDTH)
    return lax.all_to_all(copies, axes, 0, 0, tiled=True)


ACROSS = ("far", "y", "member")


def summed_along(value, axis):
    count = lax.axis_size(axis)
    return jnp.sum(gathered(value, axis).reshape(count, -1, WIDTH).astype(F32), axis=0).astype(BF)


def make_unpack_kernel(factor):
    def unpack_kernel(sum_ref, taps, conv_b, gain, offset, up, up_b, down, down_b, scale):
        for block in range(BLOCKS):
            base = block * HALF_ROWS
            for part in range(HID // WIDTH):
                rows = slice(base + part * WIDTH, base + (part + 1) * WIDTH)
                up[block, :, part * WIDTH : (part + 1) * WIDTH] = sum_ref[rows, :].astype(F32) * factor
                rows = slice(base + HID + part * WIDTH, base + HID + (part + 1) * WIDTH)
                down[block, part * WIDTH : (part + 1) * WIDTH, :] = (sum_ref[rows, :].astype(F32) * factor).T
            base += 2 * HID
            vectors = sum_ref[base : base + 16, :].astype(F32) * factor
            for row, ref in enumerate((conv_b, gain, offset, down_b, scale)):
                ref[block : block + 1, :] = vectors[row : row + 1]
            for part in range(HID // WIDTH):
                up_b[block : block + 1, part * WIDTH : (part + 1) * WIDTH] = vectors[8 + part : 9 + part]
            base += 16
            kernel_sum = sum_ref[base : base + 64, :].astype(F32) * factor
            for row in range(TAPS * TAPS):
                taps[row, block : block + 1, :] = kernel_sum[row : row + 1]

    return unpack_kernel


def laid_down(items):
    rows = sum(item.shape[0] for item in items)
    total, at = None, 0
    for item in items:
        edges = [(at, rows - at - item.shape[0], 0)] + [(0, 0, 0)] * (item.ndim - 1)
        part = lax.pad(item, jnp.zeros((), item.dtype), edges)
        total = part if total is None else total + part
        at += item.shape[0]
    return total


def shaped(*shapes):
    return [jax.ShapeDtypeStruct(shape, dtype) for shape, dtype in shapes]


def call(kernel, shapes, inputs, scratch=(), scalars=0, cost=None):
    specs = [pl.BlockSpec(memory_space=pltpu.SMEM)] * scalars + whole(len(inputs) - scalars)
    return pl.pallas_call(
        kernel,
        out_shape=shaped(*shapes),
        in_specs=specs,
        out_specs=whole(len(shapes)),
        scratch_shapes=list(scratch),
        compiler_params=kernel_params(),
        cost_estimate=cost,
    )(*inputs)


def body(
    states, cotangent, seam_codes, corner_codes, dw_kernel, dw_bias, norm_gain, norm_bias, up_weight, up_bias,
    down_weight, down_bias, layer_scale,
):
    count = lax.axis_size(TILE_AXES) * lax.axis_size("member")
    here = lax.axis_index(TILE_AXES).astype(jnp.int32).reshape(1)
    codes = jnp.concatenate([seam_codes.T, corner_codes.T])
    field = states.reshape(CELLS, WIDTH)
    upstream = cotangent.reshape(CELLS, WIDTH)
    message = ((4, MESSAGE, WIDTH), BF)
    padded_shape = ((PAD_ROWS, PAD_COLS, WIDTH), F32)
    weights_shape = ((2 * HID, WIDTH), BF)
    sums_shape = ((16, WIDTH), BF)
    cells = (CELLS, WIDTH)
    inside, edges = (INSIDE, WIDTH), (2 * EDGE, WIDTH)
    wide_sums = [((WIDTH, HID), F32), ((WIDTH, HID), F32), ((16, WIDTH), F32), ((1, HID), F32)]
    padded_scratch = pltpu.VMEM((PAD_ROWS, PAD_COLS, WIDTH), F32)
    grown_scratch = pltpu.VMEM((PAD_ROWS, GROWN_COLS, WIDTH), F32)
    cells_scratch = pltpu.VMEM(cells, F32)
    sums = [grown_scratch, *(pltpu.VMEM(*item) for item in wide_sums), pltpu.VMEM((SIZE * 8, WIDTH), F32)]
    tap_scratch = [pltpu.VMEM((64 * 8, WIDTH), F32)]
    vpu = pl.CostEstimate(flops=2 * 49 * CELLS * WIDTH, bytes_accessed=3 << 20, transcendentals=0)

    sent, gather, owners = call(
        select_kernel,
        [message, ((4 * MESSAGE, CELLS), BF), ((4, 8, MESSAGE), jnp.int32)],
        [here, codes, field],
        scalars=2,
    )
    near = beside(sent)
    packed = laid_down(
        [dw_kernel.transpose(1, 2, 0, 3).reshape(TAPS * TAPS, BLOCKS, WIDTH)]
        + [item[None] for item in (dw_bias, norm_gain, norm_bias, down_bias, layer_scale)]
        + [up_bias.reshape(BLOCKS, HID // WIDTH, WIDTH).transpose(1, 0, 2)]
    )
    near, packed = lax.optimization_barrier((near, packed))
    params = (packed, up_weight, down_weight)
    far = beyond(sent, *near)
    part, conv_part = call(
        first_inside_kernel,
        [(inside, BF), (inside, F32)],
        [here, field, *near, *params],
        [padded_scratch, cells_scratch],
        scalars=1,
        cost=vpu,
    )
    middle, conv_edges, padded_0, sent = call(
        first_kernel,
        [(cells, BF), (edges, F32), padded_shape, message],
        [here, field, *far, *near, part, gather, *params],
        [cells_scratch],
        scalars=1,
    )
    near = beside(sent)
    (scatter,) = call(scatter_kernel, [((CELLS, 4 * MESSAGE), BF)], [owners], cost=vpu)
    near, scatter = lax.optimization_barrier((near, scatter))
    far = beyond(sent, *near)
    out_part, *partial = call(
        second_inside_kernel,
        [(inside, BF), (inside, F32), *wide_sums],
        [here, middle, *near, upstream, *params],
        [padded_scratch, cells_scratch],
        scalars=1,
        cost=vpu,
    )
    out_edges, padded_1, grad_1, sent, weights_1, sums_1 = call(
        second_kernel,
        [(edges, BF), padded_shape, (cells, F32), message, weights_shape, sums_shape],
        [here, middle, *far, *near, *partial, upstream, *params],
        [cells_scratch, *sums],
        scalars=1,
    )
    near = beside(sent)
    taps_1, out = call(
        taps_and_out_kernel,
        [((64, WIDTH), BF), (cells, BF)],
        [padded_1, grad_1, out_part, out_edges],
        tap_scratch,
        cost=vpu,
    )
    near, taps_1 = lax.optimization_barrier((near, taps_1))
    far = beyond(sent, *near)
    (inner_1,) = call(make_inner_kernel(1), [(cells, F32)], [grad_1, packed], [grown_scratch], cost=vpu)
    saved = call(
        third_again_kernel,
        [(cells, F32), (cells, F32), (cells, BF), ((CELLS, HID), BF), ((CELLS, HID), F32), (cells, F32)],
        [conv_part, conv_edges, *params],
        [cells_scratch],
        cost=vpu,
    )
    far, inner_1, saved = lax.optimization_barrier((far, inner_1, saved))
    upstream_0, grad_0, sent, weights_0, sums_0 = call(
        third_kernel,
        [(cells, F32), (cells, F32), message, weights_shape, sums_shape],
        [here, *saved, upstream, inner_1, *far, *near, scatter, *params],
        sums,
        scalars=1,
    )
    near = beside(sent)
    core = lax.axis_index("core").astype(jnp.int32).reshape(1)
    kept, given = call(
        halves_kernel,
        [((HALF_ROWS, WIDTH), BF), ((HALF_ROWS, WIDTH), BF)],
        [core, padded_0, grad_0, weights_0, sums_0, weights_1, sums_1, taps_1],
        [pltpu.VMEM((64, WIDTH), BF), *tap_scratch],
        scalars=1,
    )
    total = (kept.astype(F32) + swapped(given, "core").astype(F32)).astype(BF)
    total = summed_apart(total, ACROSS)
    total, near = lax.optimization_barrier((total, near))
    far = beyond(sent, *near)
    (inner_0,) = call(make_inner_kernel(0), [(cells, F32)], [grad_0, packed], [grown_scratch], cost=vpu)
    total = gathered(summed_along(total, "z"), ACROSS)
    total, far, inner_0 = lax.optimization_barrier((total, far, inner_0))
    (grad_field,) = call(last_kernel, [(cells, BF)], [upstream_0, inner_0, *far, *near, scatter])
    total = joined(total, "core")
    row, wide = ((BLOCKS, WIDTH), F32), ((BLOCKS, HID), F32)
    grads = call(
        make_unpack_kernel(1.0 / math.sqrt(count * CELLS)),
        [
            ((TAPS * TAPS, BLOCKS, WIDTH), F32), row, row, row, ((BLOCKS, WIDTH, HID), F32), wide,
            ((BLOCKS, HID, WIDTH), F32), row, row,
        ],
        [total],
    )
    kernel_grad = grads[0].reshape(TAPS, TAPS, BLOCKS, WIDTH).transpose(2, 0, 1, 3)
    shape = states.shape
    return (out.reshape(shape), grad_field.reshape(shape), kernel_grad, *grads[1:])


def solution(mesh):
    split = Mesh(mesh.devices.reshape(2, 4, 8, 2, 2), (*TILE_AXES, "member"))
    field = P("member", TILE_AXES, None, None, None)
    return jax.shard_map(
        body,
        mesh=split,
        in_specs=(field, field) + (P(),) * 11,
        out_specs=(field, field) + (P(),) * 9,
        check_vma=False,
    )
```

```python
import math

import jax
import jax.numpy as jnp
from jax import lax
from jax.experimental import pallas as pl
from jax.experimental.pallas import tpu as pltpu
from jax.sharding import Mesh, PartitionSpec as P

BF = jnp.bfloat16
F32 = jnp.float32
BLOCKS = 2
SIZE = 32
CELLS = SIZE * SIZE
WIDTH = 128
HID = 512
TAPS = 7
CHUNK = 256
PAD_ROWS = 38
PAD_COLS = 48
GROWN_COLS = 64
MESSAGE = 128
TILES = 128
PARAM_ROWS = 58
EPSILON = 1e-06
GELU_C = 0.7978845608028654
GELU_A = 0.044715
TILE_AXES = ("far", "y", "z", "core")
VMEM_LIMIT = 16 * 1024 * 1024


def kernel_params():
    return pltpu.CompilerParams(vmem_limit_bytes=VMEM_LIMIT)


def whole(count):
    return [pl.BlockSpec(memory_space=pltpu.VMEM)] * count


def onehot(condition):
    return jnp.where(condition, 1.0, 0.0).astype(BF)


def matmul(left, right, dims=((1,), (0,))):
    return lax.dot_general(left, right, (dims, ((), ())), preferred_element_type=F32)


def strip_cells(code, slot, facing):
    along = slot & 31
    depth = slot >> 5
    depth = 2 - depth if facing in (0, 2) else depth
    edge = code & 3
    along = jnp.where(code >= 4, 31 - along, along)
    depth = jnp.where((edge & 1) == 1, 31 - depth, depth)
    return jnp.where(edge < 2, depth * SIZE + along, along * SIZE + depth)


def corner_cells(first, second, slot):
    at = jnp.where(slot < 112, slot - 96, slot - 112)
    code = jnp.where(slot < 112, first, second)
    row = (at * 11) >> 5
    col = at - 3 * row
    block = (row + 29 * (code >> 1)) * SIZE + col + 29 * (code & 1)
    return jnp.where((at >= 0) & (at < 9) & (code < 4), block, -1)


def side_of(here, shift):
    return (here >> shift) & 1


def slot_of_facing(here, facing):
    row_side, col_side = side_of(here, 2), side_of(here, 0)
    return (row_side, 1 - row_side, 2 + col_side, 3 - col_side)[facing]


def seam_of(codes_ref, here, facing):
    step = (4, -4, 1, -1)[facing]
    return codes_ref[facing, (here + step) & (TILES - 1)]


def corner_of(codes_ref, here, step, direction):
    return codes_ref[4 + direction, (here + step) & (TILES - 1)]


def gathered_cells(codes_ref, here, facing, slot):
    strip = strip_cells(seam_of(codes_ref, here, facing), slot, facing)
    if facing < 2:
        return jnp.where(slot < 96, strip, -1)
    if facing == 2:
        below, above = corner_of(codes_ref, here, 5, 0), corner_of(codes_ref, here, -3, 2)
        flip = side_of(here + 1, 2)
    else:
        below, above = corner_of(codes_ref, here, 3, 1), corner_of(codes_ref, here, -5, 3)
        flip = side_of(here - 1, 2)
    first, second = jnp.where(flip == 0, below, above), jnp.where(flip == 0, above, below)
    return jnp.where(slot < 96, strip, corner_cells(first, second, slot))


def scattered_cells(codes_ref, here, facing, slot):
    strip = strip_cells(seam_of(codes_ref, here, facing), slot, facing)
    if facing >= 2:
        return jnp.where(slot < 96, strip, -1)
    if facing == 0:
        right, left = corner_of(codes_ref, here, 5, 0), corner_of(codes_ref, here, 3, 1)
    else:
        right, left = corner_of(codes_ref, here, -3, 2), corner_of(codes_ref, here, -5, 3)
    flip = side_of(here, 0)
    first, second = jnp.where(flip == 0, right, left), jnp.where(flip == 0, left, right)
    return jnp.where(slot < 96, strip, corner_cells(first, second, slot))


def select_kernel(here_ref, codes_ref, field_ref, sent_ref, gather_ref, owners_ref):
    here = here_ref[0]
    slot = iota((MESSAGE, WIDTH), 0)
    lane = iota((MESSAGE, WIDTH), 1)
    for facing in range(4):
        cells = gathered_cells(codes_ref, here, facing, slot)
        for part in range(CELLS // WIDTH):
            chosen = onehot(cells == lane + part * WIDTH)
            gather_ref[facing * MESSAGE : (facing + 1) * MESSAGE, part * WIDTH : (part + 1) * WIDTH] = chosen
    slot = iota((8, MESSAGE), 1)
    for facing in range(4):
        owners_ref[slot_of_facing(here, facing)] = scattered_cells(codes_ref, here, facing, slot)
    send_cells(here, gather_ref[...], field_ref[...], sent_ref)


def send_cells(here, gather, field, sent_ref):
    sent = matmul(gather, field).astype(BF)
    for facing in range(4):
        sent_ref[slot_of_facing(here, facing)] = sent[facing * MESSAGE : (facing + 1) * MESSAGE]


def scatter_kernel(owners_ref, scatter_ref):
    cell = iota((CELLS, MESSAGE), 0)
    for slot in range(4):
        scatter_ref[:, slot * MESSAGE : (slot + 1) * MESSAGE] = onehot(cell == owners_ref[slot][0:1])


def row_rim_slots(position, strip, left=None, right=None):
    depth = jnp.where(position >= 96, 2, jnp.where(position >= 48, 1, 0))
    along = position - 48 * depth - 5
    slot = jnp.full_like(position, -1)
    if strip:
        slot = jnp.where((along >= 3) & (along < 35), 32 * depth + along - 3, slot)
    if left is not None:
        slot = jnp.where((along >= 0) & (along < 3), left + 3 * depth + along, slot)
    if right is not None:
        slot = jnp.where((along >= 35) & (along < 38), right + 3 * depth + along - 35, slot)
    return slot


def col_rim_slots(position, first):
    depth = (position & 7) - first
    slot = 32 * depth + (position >> 3)
    return jnp.where((depth >= 0) & (depth < 3), slot, -1)


def iota(shape, dim):
    return lax.broadcasted_iota(jnp.int32, shape, dim)


def fill_inside(inside_ref, here, field, by_a, by_b):
    side = side_of(here, 0)
    west, east = jnp.where(side == 0, by_b, by_a), jnp.where(side == 0, by_a, by_b)
    cols = (SIZE * 8, MESSAGE)
    place = onehot(col_rim_slots(iota(cols, 0), 5) == iota(cols, 1))
    inside_ref[:, 0:8] = matmul(place, west).reshape(SIZE, 8, WIDTH)
    place = onehot(col_rim_slots(iota(cols, 0), 0) == iota(cols, 1))
    inside_ref[:, 40:48] = matmul(place, east).reshape(SIZE, 8, WIDTH)
    inside_ref[:, 8:40] = field.astype(F32).reshape(SIZE, SIZE, WIDTH)


def fill_ends(ends_ref, rims_ref, here, inside_ref, by_c, by_d):
    row_side, col_side = side_of(here, 2), side_of(here, 0)
    north, south = jnp.where(row_side == 0, by_d, by_c), jnp.where(row_side == 0, by_c, by_d)
    rows = (3 * PAD_COLS, MESSAGE)
    slots = row_rim_slots(iota(rows, 0), True, 112 - 16 * col_side, 96 + 16 * col_side)
    place = onehot(slots == iota(rows, 1))
    rims_ref[0:3] = matmul(place, north).reshape(3, PAD_COLS, WIDTH)
    rims_ref[3:6] = matmul(place, south).reshape(3, PAD_COLS, WIDTH)
    ends_ref[0:3] = rims_ref[0:3]
    ends_ref[3:10] = inside_ref[0:7]
    ends_ref[10:17] = inside_ref[25:32]
    ends_ref[17:20] = rims_ref[3:6]


def convolve_ends(ends_ref, params, bias, conv_ref):
    convolve(ends_ref, 5, params, False, bias, conv_ref, 0, 1)
    convolve(ends_ref, 5, params, False, bias, conv_ref, 7, 8, 18)


def tap(kernel, row_tap, col_tap):
    ref, block = kernel
    return ref[row_tap * TAPS + col_tap, block : block + 1, :]


def convolve(source_ref, first_col, kernel_ref, flipped, start, out_ref, first=0, last=SIZE // 4, shift=0):
    def group(index, carry):
        totals = [jnp.broadcast_to(start, (SIZE, WIDTH)) for _ in range(4)]
        for col_tap in range(TAPS):
            for row in range(4 + TAPS - 1):
                values = source_ref[index * 4 + row - shift, first_col + col_tap : first_col + col_tap + SIZE, :]
                for out in range(max(0, row - TAPS + 1), min(4, row + 1)):
                    a, e = row - out, col_tap
                    if flipped:
                        a, e = TAPS - 1 - a, TAPS - 1 - e
                    totals[out] = totals[out] + values * tap(kernel_ref, a, e)
        for out in range(4):
            out_ref[pl.ds(pl.multiple_of(index * 128 + out * SIZE, SIZE), SIZE), :] = totals[out]
        return carry

    lax.fori_loop(first, last, group, 0)


def kernel_sums(padded_ref, grad_ref, sums_ref):
    sums_ref[...] = jnp.zeros_like(sums_ref)

    def group(index, carry):
        grads = [
            grad_ref[pl.ds(pl.multiple_of(index * 128 + row * SIZE, SIZE), SIZE), :] for row in range(4)
        ]
        for col_tap in range(TAPS):
            totals = [jnp.zeros((8, WIDTH), F32) for _ in range(TAPS)]
            for row in range(4 + TAPS - 1):
                values = padded_ref[index * 4 + row, 5 + col_tap : 5 + col_tap + SIZE, :]
                for out in range(max(0, row - TAPS + 1), min(4, row + 1)):
                    product = values * grads[out]
                    totals[row - out] = totals[row - out] + (
                        (product[0:8] + product[8:16]) + (product[16:24] + product[24:32])
                    )
            for row_tap in range(TAPS):
                at = 8 * (row_tap * TAPS + col_tap)
                sums_ref[at : at + 8, :] += totals[row_tap]
        return carry

    lax.fori_loop(0, SIZE // 4, group, 0)


def row_rim(grown_ref, kernel_ref, top):
    rows = []
    for depth in range(3):
        total = jnp.zeros((PAD_COLS, WIDTH), F32)
        for row_tap in range(TAPS):
            source = depth - row_tap if top else 35 + depth - row_tap
            if 0 <= source < SIZE:
                for col_tap in range(TAPS):
                    at = 11 - col_tap
                    total = total + grown_ref[source + 3, at : at + PAD_COLS, :] * tap(kernel_ref, row_tap, col_tap)
        rows.append(total)
    return jnp.concatenate(rows, axis=0)


def col_rim(grown_ref, kernel_ref, left, out_ref):
    def group(index, carry):
        totals = [jnp.zeros((8, WIDTH), F32) for _ in range(8)]
        for col_tap in range(3) if left else range(4, TAPS):
            at = 11 - col_tap if left else 51 - col_tap
            for row in range(8 + TAPS - 1):
                values = grown_ref[index * 8 + row, at : at + 8, :]
                for out in range(max(0, row - TAPS + 1), min(8, row + 1)):
                    totals[out] = totals[out] + values * tap(kernel_ref, TAPS - 1 - (row - out), col_tap)
        for out in range(8):
            out_ref[pl.ds(pl.multiple_of(index * 64 + out * 8, 8), 8), :] = totals[out]
        return carry

    lax.fori_loop(0, SIZE // 8, group, 0)


def send_rims(here, grown_ref, kernel, rim_ref, sent_ref):
    rows = (MESSAGE, 3 * PAD_COLS)
    place = onehot(row_rim_slots(iota(rows, 1), True) == iota(rows, 0))
    rims = []
    for facing in range(2):
        rim = row_rim(grown_ref, kernel, facing == 0).astype(BF)
        sent_ref[(1 - side_of(here, 2), side_of(here, 2))[facing]] = matmul(place, rim).astype(BF)
        rims.append(rim)
    cols = (MESSAGE, SIZE * 8)
    for left in (True, False):
        col_rim(grown_ref, kernel, left, rim_ref)
        place = onehot(col_rim_slots(iota(cols, 1), 5 if left else 0) == iota(cols, 0))
        message = matmul(place, rim_ref[...].astype(BF))
        flip = side_of(here - 1 if left else here + 1, 2)
        for rim, base in ((rims[0], 112 - 16 * flip), (rims[1], 96 + 16 * flip)):
            slots = row_rim_slots(iota(rows, 1), False, base if left else None, None if left else base)
            message = message + matmul(onehot(slots == iota(rows, 0)), rim)
        side = side_of(here, 0)
        sent_ref[3 - side if left else 2 + side] = message.astype(BF)


def normalised(conv):
    centred = conv - jnp.mean(conv, axis=1, keepdims=True)
    inv_std = lax.rsqrt(jnp.mean(centred * centred, axis=1, keepdims=True) + EPSILON)
    return centred * inv_std, inv_std


def forward_chunk(conv, field, rows, up_w, up_b, down_w):
    gain, offset, down_b, scale = rows
    standard, _ = normalised(conv)
    normed = (standard * gain + offset).astype(BF)
    pre = matmul(normed, up_w) + up_b
    tangent = jnp.tanh(pre * (GELU_C + (GELU_C * GELU_A) * pre * pre))
    activated = (0.5 * pre * (1.0 + tangent)).astype(BF)
    branch = matmul(activated, down_w) + down_b
    return (field.astype(F32) + scale * branch).astype(BF)


def block_rows(params_ref, block):
    rows = [params_ref[row, block : block + 1, :] for row in range(TAPS * TAPS, PARAM_ROWS)]
    return (*rows[:5], jnp.concatenate(rows[5:], axis=1))


EDGE = 4 * SIZE
INSIDE = CELLS - 2 * EDGE


def first_inside_kernel(
    here_ref, field_ref, a_ref, b_ref, params_ref, up_ref, down_ref,
    out_ref, conv_ref, inside_ref, full_ref,
):
    fill_inside(inside_ref, here_ref[0], field_ref[...], a_ref[...], b_ref[...])
    bias, gain, offset, down_b, scale, up_b = block_rows(params_ref, 0)
    convolve(inside_ref, 5, (params_ref, 0), False, bias, full_ref, 1, 7, 3)

    def chunk(index, carry):
        at = pl.ds(pl.multiple_of(index * CHUNK, CHUNK), CHUNK)
        cells = pl.ds(pl.multiple_of(EDGE + index * CHUNK, EDGE), CHUNK)
        conv = full_ref[cells, :]
        conv_ref[at, :] = conv
        out_ref[at, :] = forward_chunk(
            conv, field_ref[cells, :], (gain, offset, down_b, scale), up_ref[0], up_b, down_ref[0]
        )
        return carry

    lax.fori_loop(0, INSIDE // CHUNK, chunk, 0, unroll=True)


def ends(ref):
    return jnp.concatenate([ref[:EDGE, :], ref[CELLS - EDGE :, :]], axis=0)


def join_rows(ref, inside, edges):
    ref[:EDGE, :] = edges[:EDGE]
    ref[EDGE : CELLS - EDGE, :] = inside
    ref[CELLS - EDGE :, :] = edges[EDGE:]


def first_kernel(
    here_ref, field_ref, c_ref, d_ref, inside_ref, out_in_ref, gather_ref, params_ref, up_ref, down_ref,
    out_ref, conv_ref, rims_ref, sent_ref, ends_ref, full_ref,
):
    here = here_ref[0]
    fill_ends(ends_ref, rims_ref, here, inside_ref, c_ref[...], d_ref[...])
    bias, gain, offset, down_b, scale, up_b = block_rows(params_ref, 0)
    convolve_ends(ends_ref, (params_ref, 0), bias, full_ref)
    conv = ends(full_ref)
    conv_ref[...] = conv
    out = forward_chunk(conv, ends(field_ref), (gain, offset, down_b, scale), up_ref[0], up_b, down_ref[0])
    join_rows(out_ref, out_in_ref[...], out)
    send_cells(here, gather_ref[...], out_ref[...], sent_ref)


def again(block, conv, refs):
    params_ref, up_ref, down_ref = refs
    _, gain, offset, down_b, _, up_b = block_rows(params_ref, block)
    standard, inv_std = normalised(conv)
    normed = (standard * gain + offset).astype(BF)
    pre = matmul(normed, up_ref[block]) + up_b
    square = pre * pre
    tangent = jnp.tanh(pre * (GELU_C + (GELU_C * GELU_A) * square))
    half = 0.5 + 0.5 * tangent
    activated = (pre * half).astype(BF)
    slope = half + pre * (0.5 - 0.5 * tangent * tangent) * (GELU_C + (3.0 * GELU_C * GELU_A) * square)
    branch = matmul(activated, down_ref[block]) + down_b
    return standard, inv_std, normed, activated, slope, branch


def backward_chunk(block, saved, upstream, refs):
    params_ref, up_ref, down_ref, up_sum, down_sum, vector_sum, up_b_sum = refs
    standard, inv_std, normed, activated, slope, branch = saved
    _, gain, _, _, scale, _ = block_rows(params_ref, block)
    scaled = upstream * scale
    scaled_b = scaled.astype(BF)
    down_sum[...] += matmul(scaled_b, activated, ((0,), (0,)))
    pre_grad = matmul(scaled_b, down_ref[block], ((1,), (1,))) * slope
    up_b_sum[...] += jnp.sum(pre_grad, axis=0, keepdims=True)
    pre_grad_b = pre_grad.astype(BF)
    up_sum[...] += matmul(normed, pre_grad_b, ((0,), (0,)))
    normed_grad = matmul(pre_grad_b, up_ref[block], ((1,), (1,)))
    std_grad = normed_grad * gain
    conv_grad = inv_std * (
        std_grad
        - jnp.mean(std_grad, axis=1, keepdims=True)
        - standard * jnp.mean(std_grad * standard, axis=1, keepdims=True)
    )
    for row, values in enumerate((conv_grad, normed_grad * standard, normed_grad, scaled, upstream * branch)):
        vector_sum[row : row + 1, :] += jnp.sum(values, axis=0, keepdims=True)
    return conv_grad


def through(block, conv, upstream, field, refs):
    saved = again(block, conv, refs[:3])
    scale = block_rows(refs[0], block)[4]
    out = (field.astype(F32) + scale * saved[5]).astype(BF)
    return backward_chunk(block, saved, upstream, refs), out


def clear(refs):
    for ref in refs:
        ref[...] = jnp.zeros_like(ref)


def fill_grown(grown_ref, grad):
    grown_ref[0:3] = jnp.zeros((3, GROWN_COLS, WIDTH), F32)
    grown_ref[35:38] = jnp.zeros((3, GROWN_COLS, WIDTH), F32)
    grown_ref[3:35, 0:16] = jnp.zeros((SIZE, 16, WIDTH), F32)
    grown_ref[3:35, 48:64] = jnp.zeros((SIZE, 16, WIDTH), F32)
    grown_ref[3:35, 16:48] = grad.reshape(SIZE, SIZE, WIDTH)


def pack_sums(refs, weights_ref, vectors_ref):
    up_sum, down_sum, vector_sum, up_b_sum = refs[3:]
    for part in range(HID // WIDTH):
        lanes = slice(part * WIDTH, (part + 1) * WIDTH)
        weights_ref[part * WIDTH : (part + 1) * WIDTH, :] = up_sum[:, lanes].astype(BF)
        weights_ref[HID + part * WIDTH : HID + (part + 1) * WIDTH, :] = down_sum[:, lanes].astype(BF)
        vector_sum[8 + part : 9 + part, :] = up_b_sum[:, lanes]
    vectors_ref[...] = vector_sum[...].astype(BF)


def second_inside_kernel(
    here_ref, field_ref, a_ref, b_ref, cotangent_ref, params_ref, up_ref, down_ref,
    out_ref, inside_ref, grad_ref, up_sum, down_sum, vector_sum, up_b_sum, conv_ref,
):
    fill_inside(inside_ref, here_ref[0], field_ref[...], a_ref[...], b_ref[...])
    convolve(inside_ref, 5, (params_ref, 1), False, block_rows(params_ref, 1)[0], conv_ref, 1, 7, 3)
    refs = (params_ref, up_ref, down_ref, up_sum, down_sum, vector_sum, up_b_sum)
    clear(refs[3:])

    def chunk(index, carry):
        at = pl.ds(pl.multiple_of(index * CHUNK, CHUNK), CHUNK)
        cells = pl.ds(pl.multiple_of(EDGE + index * CHUNK, EDGE), CHUNK)
        grad_ref[at, :], out_ref[at, :] = through(
            1, conv_ref[cells, :], cotangent_ref[cells, :].astype(F32), field_ref[cells, :], refs
        )
        return carry

    lax.fori_loop(0, INSIDE // CHUNK, chunk, 0, unroll=True)


def second_kernel(
    here_ref, field_ref, c_ref, d_ref, inside_ref, grad_in_ref, up_in, down_in, vector_in, up_b_in,
    cotangent_ref, params_ref, up_ref, down_ref,
    out_ref, rims_ref, grad_ref, sent_ref, weights_ref, sums_ref,
    ends_ref, conv_ref, grown_ref, up_sum, down_sum, vector_sum, up_b_sum, rim_ref,
):
    here = here_ref[0]
    fill_ends(ends_ref, rims_ref, here, inside_ref, c_ref[...], d_ref[...])
    convolve_ends(ends_ref, (params_ref, 1), block_rows(params_ref, 1)[0], conv_ref)
    refs = (params_ref, up_ref, down_ref, up_sum, down_sum, vector_sum, up_b_sum)
    for ref, start in zip(refs[3:], (up_in, down_in, vector_in, up_b_in)):
        ref[...] = start[...]
    grad, out_ref[...] = through(1, ends(conv_ref), ends(cotangent_ref).astype(F32), ends(field_ref), refs)
    join_rows(grad_ref, grad_in_ref[...], grad)
    fill_grown(grown_ref, grad_ref[...])
    send_rims(here, grown_ref, (params_ref, 1), rim_ref, sent_ref)
    pack_sums(refs, weights_ref, sums_ref)


def third_again_kernel(
    conv_ref, conv_edge_ref, params_ref, up_ref, down_ref,
    standard_ref, inv_std_ref, normed_ref, activated_ref, slope_ref, branch_ref, full_ref,
):
    join_rows(full_ref, conv_ref[...], conv_edge_ref[...])

    def chunk(index, carry):
        at = pl.ds(pl.multiple_of(index * CHUNK, CHUNK), CHUNK)
        saved = again(0, full_ref[at, :], (params_ref, up_ref, down_ref))
        standard_ref[at, :], _, normed_ref[at, :], activated_ref[at, :], slope_ref[at, :], branch_ref[at, :] = saved
        inv_std_ref[at, :] = jnp.broadcast_to(saved[1], (CHUNK, WIDTH))
        return carry

    lax.fori_loop(0, CELLS // CHUNK, chunk, 0, unroll=True)


def third_kernel(
    here_ref, standard_ref, inv_std_ref, normed_ref, activated_ref, slope_ref, branch_ref, base_ref, c_ref, d_ref,
    scatter_ref, params_ref, up_ref, down_ref,
    upstream_ref, grad_ref, sent_ref, weights_ref, sums_ref,
    grown_ref, up_sum, down_sum, vector_sum, up_b_sum, rim_ref,
):
    upstream_ref[...] = base_ref[...] + owned(scatter_ref, 0, c_ref, d_ref)
    refs = (params_ref, up_ref, down_ref, up_sum, down_sum, vector_sum, up_b_sum)
    clear(refs[3:])
    saved_refs = (standard_ref, inv_std_ref, normed_ref, activated_ref, slope_ref, branch_ref)

    def chunk(index, carry):
        at = pl.ds(pl.multiple_of(index * CHUNK, CHUNK), CHUNK)
        grad_ref[at, :] = backward_chunk(0, [ref[at, :] for ref in saved_refs], upstream_ref[at, :], refs)
        return carry

    lax.fori_loop(0, CELLS // CHUNK, chunk, 0, unroll=True)
    fill_grown(grown_ref, grad_ref[...])
    send_rims(here_ref[0], grown_ref, (params_ref, 0), rim_ref, sent_ref)
    pack_sums(refs, weights_ref, sums_ref)


def owned(scatter_ref, first, *refs):
    lanes = slice(first * MESSAGE, (first + len(refs)) * MESSAGE)
    return matmul(scatter_ref[:, lanes], jnp.concatenate([ref[...] for ref in refs], axis=0))


def last_kernel(base_ref, c_ref, d_ref, scatter_ref, out_ref):
    out_ref[...] = (base_ref[...] + owned(scatter_ref, 0, c_ref, d_ref)).astype(BF)


def make_inner_kernel(block):
    def inner_kernel(grad_ref, upstream_ref, a_ref, b_ref, scatter_ref, params_ref, base_ref, grown_ref):
        fill_grown(grown_ref, grad_ref[...])
        convolve(grown_ref, 13, (params_ref, block), True, jnp.zeros((1, WIDTH), F32), base_ref)
        base_ref[...] += upstream_ref[...].astype(F32) + owned(scatter_ref, 2, a_ref, b_ref)

    return inner_kernel


def fill_padded(padded_ref, inside_ref, rims_ref):
    padded_ref[0:3] = rims_ref[0:3]
    padded_ref[3:35] = inside_ref[...]
    padded_ref[35:38] = rims_ref[3:6]


def taps_and_out_kernel(
    pad_inside_ref, pad_rims_ref, grad_ref, inside_ref, edges_ref, taps_ref, out_ref, padded_ref, sums_ref
):
    join_rows(out_ref, inside_ref[...], edges_ref[...])
    fill_padded(padded_ref, pad_inside_ref, pad_rims_ref)
    taps_kernel(padded_ref, grad_ref, taps_ref, sums_ref)


def taps_kernel(padded_ref, grad_ref, taps_ref, sums_ref):
    kernel_sums(padded_ref, grad_ref, sums_ref)
    taps_ref[...] = jnp.sum(sums_ref[...].reshape(64, 8, WIDTH), axis=1).astype(BF)


def halves_kernel(
    core_ref, pad_inside_ref, pad_rims_ref, grad_ref, weights_0_ref, sums_0_ref, weights_1_ref, sums_1_ref, taps_1_ref,
    kept_ref, given_ref, taps_ref, padded_ref, partial_ref,
):
    fill_padded(padded_ref, pad_inside_ref, pad_rims_ref)
    taps_kernel(padded_ref, grad_ref, taps_ref, partial_ref)

    def fill(half_ref, *parts):
        at = 0
        for part in parts:
            half_ref[at : at + part.shape[0], :] = part[...]
            at += part.shape[0]
        half_ref[at:, :] = jnp.zeros((HALF_ROWS - at, WIDTH), BF)

    first = (weights_0_ref, sums_0_ref, taps_ref)
    second = (weights_1_ref, sums_1_ref, taps_1_ref)
    for core, kept, given in ((0, first, second), (1, second, first)):

        @pl.when(core_ref[0] == core)
        def _(kept=kept, given=given):
            fill(kept_ref, *kept)
            fill(given_ref, *given)


def swapped_tiles(value, step, odd):
    starts = [tile for tile in range(TILES) if (tile // step) % 2 == odd]
    pairs = [(tile, (tile + step) % TILES) for tile in starts]
    return lax.ppermute(value, TILE_AXES, pairs + [(target, source) for source, target in pairs])


def beside(sent):
    by_b = swapped_tiles(sent[3], 1, 1)
    return swapped_tiles(sent[2], 1, 0), by_b


def beyond(sent, by_a, by_b):
    by_c = swapped_tiles(jnp.concatenate([sent[0, :96], by_a[96:112], by_b[96:112]]), 4, 0)
    by_d = swapped_tiles(jnp.concatenate([sent[1, :96], by_a[112:], by_b[112:]]), 4, 1)
    return by_c, by_d


HALF_ROWS = 1152


def swapped(value, axis):
    return lax.ppermute(value, axis, [(0, 1), (1, 0)])


def summed_apart(value, axes):
    count = lax.axis_size(axes)
    parts = lax.all_to_all(value, axes, 0, 0, tiled=True).reshape(count, -1, WIDTH)
    return jnp.sum(parts.astype(F32), axis=0).astype(BF)


def gathered(value, axes):
    count = lax.axis_size(axes)
    copies = jnp.broadcast_to(value[None], (count,) + value.shape).reshape(-1, WIDTH)
    return lax.all_to_all(copies, axes, 0, 0, tiled=True)


ACROSS = ("far", "y", "member")


def summed_along(value, axis):
    count = lax.axis_size(axis)
    return jnp.sum(gathered(value, axis).reshape(count, -1, WIDTH).astype(F32), axis=0).astype(BF)


def make_unpack_kernel(factor):
    def unpack_kernel(core_ref, mine_ref, other_ref, taps, conv_b, gain, offset, up, up_b, down, down_b, scale):
        def unpack(sum_ref, block):
            for part in range(HID // WIDTH):
                rows = slice(part * WIDTH, (part + 1) * WIDTH)
                up[block, :, part * WIDTH : (part + 1) * WIDTH] = sum_ref[rows, :].astype(F32) * factor
                rows = slice(HID + part * WIDTH, HID + (part + 1) * WIDTH)
                down[block, part * WIDTH : (part + 1) * WIDTH, :] = (sum_ref[rows, :].astype(F32) * factor).T
            base = 2 * HID
            vectors = sum_ref[base : base + 16, :].astype(F32) * factor
            for row, ref in enumerate((conv_b, gain, offset, down_b, scale)):
                ref[block : block + 1, :] = vectors[row : row + 1]
            for part in range(HID // WIDTH):
                up_b[block : block + 1, part * WIDTH : (part + 1) * WIDTH] = vectors[8 + part : 9 + part]
            base += 16
            kernel_sum = sum_ref[base : base + 64, :].astype(F32) * factor
            for row in range(TAPS * TAPS):
                taps[row, block : block + 1, :] = kernel_sum[row : row + 1]

        for core in range(2):

            @pl.when(core_ref[0] == core)
            def _(core=core):
                unpack(mine_ref, core)
                unpack(other_ref, 1 - core)

    return unpack_kernel


def laid_down(items):
    rows = sum(item.shape[0] for item in items)
    total, at = None, 0
    for item in items:
        edges = [(at, rows - at - item.shape[0], 0)] + [(0, 0, 0)] * (item.ndim - 1)
        part = lax.pad(item, jnp.zeros((), item.dtype), edges)
        total = part if total is None else total + part
        at += item.shape[0]
    return total


def shaped(*shapes):
    return [jax.ShapeDtypeStruct(shape, dtype) for shape, dtype in shapes]


def call(kernel, shapes, inputs, scratch=(), scalars=0, cost=None):
    specs = [pl.BlockSpec(memory_space=pltpu.SMEM)] * scalars + whole(len(inputs) - scalars)
    return pl.pallas_call(
        kernel,
        out_shape=shaped(*shapes),
        in_specs=specs,
        out_specs=whole(len(shapes)),
        scratch_shapes=list(scratch),
        compiler_params=kernel_params(),
        cost_estimate=cost,
    )(*inputs)


def body(
    states, cotangent, seam_codes, corner_codes, dw_kernel, dw_bias, norm_gain, norm_bias, up_weight, up_bias,
    down_weight, down_bias, layer_scale,
):
    count = lax.axis_size(TILE_AXES) * lax.axis_size("member")
    here = lax.axis_index(TILE_AXES).astype(jnp.int32).reshape(1)
    field = states.reshape(CELLS, WIDTH)
    upstream = cotangent.reshape(CELLS, WIDTH)
    message = ((4, MESSAGE, WIDTH), BF)
    inside_shape = ((SIZE, PAD_COLS, WIDTH), F32)
    rims_shape = ((6, PAD_COLS, WIDTH), F32)
    ends_scratch = pltpu.VMEM((20, PAD_COLS, WIDTH), F32)
    weights_shape = ((2 * HID, WIDTH), BF)
    sums_shape = ((16, WIDTH), BF)
    cells = (CELLS, WIDTH)
    inside, edges = (INSIDE, WIDTH), (2 * EDGE, WIDTH)
    wide_sums = [((WIDTH, HID), F32), ((WIDTH, HID), F32), ((16, WIDTH), F32), ((1, HID), F32)]
    padded_scratch = pltpu.VMEM((PAD_ROWS, PAD_COLS, WIDTH), F32)
    grown_scratch = pltpu.VMEM((PAD_ROWS, GROWN_COLS, WIDTH), F32)
    cells_scratch = pltpu.VMEM(cells, F32)
    sums = [grown_scratch, *(pltpu.VMEM(*item) for item in wide_sums), pltpu.VMEM((SIZE * 8, WIDTH), F32)]
    tap_scratch = [pltpu.VMEM((64 * 8, WIDTH), F32)]
    vpu = pl.CostEstimate(flops=2 * 49 * CELLS * WIDTH, bytes_accessed=3 << 20, transcendentals=0)

    codes = jnp.concatenate([seam_codes.T, corner_codes.T])
    sent, gather, owners = call(
        select_kernel,
        [message, ((4 * MESSAGE, CELLS), BF), ((4, 8, MESSAGE), jnp.int32)],
        [here, codes, field],
        scalars=2,
    )
    near = beside(sent)
    packed = laid_down(
        [dw_kernel.transpose(1, 2, 0, 3).reshape(TAPS * TAPS, BLOCKS, WIDTH)]
        + [item[None] for item in (dw_bias, norm_gain, norm_bias, down_bias, layer_scale)]
        + [up_bias.reshape(BLOCKS, HID // WIDTH, WIDTH).transpose(1, 0, 2)]
    )
    near, packed = lax.optimization_barrier((near, packed))
    params = (packed, up_weight, down_weight)
    far = beyond(sent, *near)
    part, conv_part, pad_inside_0 = call(
        first_inside_kernel,
        [(inside, BF), (inside, F32), inside_shape],
        [here, field, *near, *params],
        [cells_scratch],
        scalars=1,
        cost=vpu,
    )
    middle, conv_edges, pad_rims_0, sent = call(
        first_kernel,
        [(cells, BF), (edges, F32), rims_shape, message],
        [here, field, *far, pad_inside_0, part, gather, *params],
        [ends_scratch, cells_scratch],
        scalars=1,
    )
    near = beside(sent)
    (scatter,) = call(scatter_kernel, [((CELLS, 4 * MESSAGE), BF)], [owners], cost=vpu)
    near, scatter = lax.optimization_barrier((near, scatter))
    far = beyond(sent, *near)
    out_part, pad_inside_1, *partial = call(
        second_inside_kernel,
        [(inside, BF), inside_shape, (inside, F32), *wide_sums],
        [here, middle, *near, upstream, *params],
        [cells_scratch],
        scalars=1,
        cost=vpu,
    )
    out_edges, pad_rims_1, grad_1, sent, weights_1, sums_1 = call(
        second_kernel,
        [(edges, BF), rims_shape, (cells, F32), message, weights_shape, sums_shape],
        [here, middle, *far, pad_inside_1, *partial, upstream, *params],
        [ends_scratch, cells_scratch, *sums],
        scalars=1,
    )
    near = beside(sent)
    taps_1, out = call(
        taps_and_out_kernel,
        [((64, WIDTH), BF), (cells, BF)],
        [pad_inside_1, pad_rims_1, grad_1, out_part, out_edges],
        [padded_scratch, *tap_scratch],
        cost=vpu,
    )
    near, taps_1 = lax.optimization_barrier((near, taps_1))
    far = beyond(sent, *near)
    (base_1,) = call(
        make_inner_kernel(1),
        [(cells, F32)],
        [grad_1, upstream, *near, scatter, packed],
        [grown_scratch],
        cost=vpu,
    )
    saved = call(
        third_again_kernel,
        [(cells, F32), (cells, F32), (cells, BF), ((CELLS, HID), BF), ((CELLS, HID), F32), (cells, F32)],
        [conv_part, conv_edges, *params],
        [cells_scratch],
        cost=vpu,
    )
    far, base_1, saved = lax.optimization_barrier((far, base_1, saved))
    upstream_0, grad_0, sent, weights_0, sums_0 = call(
        third_kernel,
        [(cells, F32), (cells, F32), message, weights_shape, sums_shape],
        [here, *saved, base_1, *far, scatter, *params],
        sums,
        scalars=1,
    )
    near = beside(sent)
    core = lax.axis_index("core").astype(jnp.int32).reshape(1)
    kept, given = call(
        halves_kernel,
        [((HALF_ROWS, WIDTH), BF), ((HALF_ROWS, WIDTH), BF)],
        [core, pad_inside_0, pad_rims_0, grad_0, weights_0, sums_0, weights_1, sums_1, taps_1],
        [pltpu.VMEM((64, WIDTH), BF), padded_scratch, *tap_scratch],
        scalars=1,
    )
    total = (kept.astype(F32) + swapped(given, "core").astype(F32)).astype(BF)
    total = summed_apart(total, ACROSS)
    total, near = lax.optimization_barrier((total, near))
    far = beyond(sent, *near)
    (base_0,) = call(
        make_inner_kernel(0),
        [(cells, F32)],
        [grad_0, upstream_0, *near, scatter, packed],
        [grown_scratch],
        cost=vpu,
    )
    total = summed_along(total, "z")
    (by_c, by_d), (total, by_c) = far, lax.optimization_barrier((total, far[0]))
    far = (by_c, by_d)
    total = gathered(total, ACROSS)
    total, far, base_0 = lax.optimization_barrier((total, far, base_0))
    (grad_field,) = call(last_kernel, [(cells, BF)], [base_0, *far, scatter])
    halves = (total, swapped(total, "core"))
    row, wide = ((BLOCKS, WIDTH), F32), ((BLOCKS, HID), F32)
    grads = call(
        make_unpack_kernel(1.0 / math.sqrt(count * CELLS)),
        [
            ((TAPS * TAPS, BLOCKS, WIDTH), F32), row, row, row, ((BLOCKS, WIDTH, HID), F32), wide,
            ((BLOCKS, HID, WIDTH), F32), row, row,
        ],
        [core, *halves],
        scalars=1,
    )
    kernel_grad = grads[0].reshape(TAPS, TAPS, BLOCKS, WIDTH).transpose(2, 0, 1, 3)
    shape = states.shape
    return (out.reshape(shape), grad_field.reshape(shape), kernel_grad, *grads[1:])


def solution(mesh):
    split = Mesh(mesh.devices.reshape(2, 4, 8, 2, 2), (*TILE_AXES, "member"))
    field = P("member", TILE_AXES, None, None, None)
    return jax.shard_map(
        body,
        mesh=split,
        in_specs=(field, field) + (P(),) * 11,
        out_specs=(field, field) + (P(),) * 9,
        check_vma=False,
    )
```

```python
import math

import jax
import jax.numpy as jnp
from jax import lax
from jax.experimental import pallas as pl
from jax.experimental.pallas import tpu as pltpu
from jax.sharding import Mesh, PartitionSpec as P

BF = jnp.bfloat16
F32 = jnp.float32
BLOCKS = 2
SIZE = 32
CELLS = SIZE * SIZE
WIDTH = 128
HID = 512
TAPS = 7
CHUNK = 256
PAD_ROWS = 38
PAD_COLS = 48
GROWN_COLS = 64
MESSAGE = 128
TILES = 128
PARAM_ROWS = 58
EPSILON = 1e-06
GELU_C = 0.7978845608028654
GELU_A = 0.044715
TILE_AXES = ("far", "y", "z", "core")
VMEM_LIMIT = 16 * 1024 * 1024


def kernel_params():
    return pltpu.CompilerParams(vmem_limit_bytes=VMEM_LIMIT)


def whole(count):
    return [pl.BlockSpec(memory_space=pltpu.VMEM)] * count


def onehot(condition):
    return jnp.where(condition, 1.0, 0.0).astype(BF)


def matmul(left, right, dims=((1,), (0,))):
    return lax.dot_general(left, right, (dims, ((), ())), preferred_element_type=F32)


def strip_cells(code, slot, facing):
    along = slot & 31
    depth = slot >> 5
    depth = 2 - depth if facing in (0, 2) else depth
    edge = code & 3
    along = jnp.where(code >= 4, 31 - along, along)
    depth = jnp.where((edge & 1) == 1, 31 - depth, depth)
    return jnp.where(edge < 2, depth * SIZE + along, along * SIZE + depth)


def corner_cells(first, second, slot):
    at = jnp.where(slot < 112, slot - 96, slot - 112)
    code = jnp.where(slot < 112, first, second)
    row = (at * 11) >> 5
    col = at - 3 * row
    block = (row + 29 * (code >> 1)) * SIZE + col + 29 * (code & 1)
    return jnp.where((at >= 0) & (at < 9) & (code < 4), block, -1)


def side_of(here, shift):
    return (here >> shift) & 1


def slot_of_facing(here, facing):
    row_side, col_side = side_of(here, 2), side_of(here, 0)
    return (row_side, 1 - row_side, 2 + col_side, 3 - col_side)[facing]


def seam_of(codes_ref, here, facing):
    step = (4, -4, 1, -1)[facing]
    return codes_ref[facing, (here + step) & (TILES - 1)]


def corner_of(codes_ref, here, step, direction):
    return codes_ref[4 + direction, (here + step) & (TILES - 1)]


def gathered_cells(codes_ref, here, facing, slot):
    strip = strip_cells(seam_of(codes_ref, here, facing), slot, facing)
    if facing < 2:
        return jnp.where(slot < 96, strip, -1)
    if facing == 2:
        below, above = corner_of(codes_ref, here, 5, 0), corner_of(codes_ref, here, -3, 2)
        flip = side_of(here + 1, 2)
    else:
        below, above = corner_of(codes_ref, here, 3, 1), corner_of(codes_ref, here, -5, 3)
        flip = side_of(here - 1, 2)
    first, second = jnp.where(flip == 0, below, above), jnp.where(flip == 0, above, below)
    return jnp.where(slot < 96, strip, corner_cells(first, second, slot))


def scattered_cells(codes_ref, here, facing, slot):
    strip = strip_cells(seam_of(codes_ref, here, facing), slot, facing)
    if facing >= 2:
        return jnp.where(slot < 96, strip, -1)
    if facing == 0:
        right, left = corner_of(codes_ref, here, 5, 0), corner_of(codes_ref, here, 3, 1)
    else:
        right, left = corner_of(codes_ref, here, -3, 2), corner_of(codes_ref, here, -5, 3)
    flip = side_of(here, 0)
    first, second = jnp.where(flip == 0, right, left), jnp.where(flip == 0, left, right)
    return jnp.where(slot < 96, strip, corner_cells(first, second, slot))


def select_kernel(here_ref, codes_ref, field_ref, sent_ref, gather_ref, owners_ref):
    here = here_ref[0]
    slot = iota((MESSAGE, WIDTH), 0)
    lane = iota((MESSAGE, WIDTH), 1)
    for facing in range(4):
        cells = gathered_cells(codes_ref, here, facing, slot)
        for part in range(CELLS // WIDTH):
            chosen = onehot(cells == lane + part * WIDTH)
            gather_ref[facing * MESSAGE : (facing + 1) * MESSAGE, part * WIDTH : (part + 1) * WIDTH] = chosen
    slot = iota((8, MESSAGE), 1)
    for facing in range(4):
        owners_ref[slot_of_facing(here, facing)] = scattered_cells(codes_ref, here, facing, slot)
    send_cells(here, gather_ref[...], field_ref[...], sent_ref)


def send_cells(here, gather, field, sent_ref):
    sent = matmul(gather, field).astype(BF)
    for facing in range(4):
        sent_ref[slot_of_facing(here, facing)] = sent[facing * MESSAGE : (facing + 1) * MESSAGE]


def scatter_kernel(owners_ref, scatter_ref):
    cell = iota((CELLS, MESSAGE), 0)
    for slot in range(4):
        scatter_ref[:, slot * MESSAGE : (slot + 1) * MESSAGE] = onehot(cell == owners_ref[slot][0:1])


def row_rim_slots(position, strip, left=None, right=None):
    depth = jnp.where(position >= 96, 2, jnp.where(position >= 48, 1, 0))
    along = position - 48 * depth - 5
    slot = jnp.full_like(position, -1)
    if strip:
        slot = jnp.where((along >= 3) & (along < 35), 32 * depth + along - 3, slot)
    if left is not None:
        slot = jnp.where((along >= 0) & (along < 3), left + 3 * depth + along, slot)
    if right is not None:
        slot = jnp.where((along >= 35) & (along < 38), right + 3 * depth + along - 35, slot)
    return slot


def col_rim_slots(position, first):
    depth = (position & 7) - first
    slot = 32 * depth + (position >> 3)
    return jnp.where((depth >= 0) & (depth < 3), slot, -1)


def iota(shape, dim):
    return lax.broadcasted_iota(jnp.int32, shape, dim)


def fill_inside(inside_ref, here, field, by_a, by_b):
    side = side_of(here, 0)
    west, east = jnp.where(side == 0, by_b, by_a), jnp.where(side == 0, by_a, by_b)
    cols = (SIZE * 8, MESSAGE)
    place = onehot(col_rim_slots(iota(cols, 0), 5) == iota(cols, 1))
    inside_ref[:, 0:8] = matmul(place, west).reshape(SIZE, 8, WIDTH)
    place = onehot(col_rim_slots(iota(cols, 0), 0) == iota(cols, 1))
    inside_ref[:, 40:48] = matmul(place, east).reshape(SIZE, 8, WIDTH)
    inside_ref[:, 8:40] = field.astype(F32).reshape(SIZE, SIZE, WIDTH)


def fill_ends(ends_ref, rims_ref, here, inside_ref, by_c, by_d):
    row_side, col_side = side_of(here, 2), side_of(here, 0)
    north, south = jnp.where(row_side == 0, by_d, by_c), jnp.where(row_side == 0, by_c, by_d)
    rows = (3 * PAD_COLS, MESSAGE)
    slots = row_rim_slots(iota(rows, 0), True, 112 - 16 * col_side, 96 + 16 * col_side)
    place = onehot(slots == iota(rows, 1))
    rims_ref[0:3] = matmul(place, north).reshape(3, PAD_COLS, WIDTH)
    rims_ref[3:6] = matmul(place, south).reshape(3, PAD_COLS, WIDTH)
    ends_ref[0:3] = rims_ref[0:3]
    ends_ref[3:10] = inside_ref[0:7]
    ends_ref[10:17] = inside_ref[25:32]
    ends_ref[17:20] = rims_ref[3:6]


def convolve_ends(ends_ref, params, bias, conv_ref):
    convolve(ends_ref, 5, params, False, bias, conv_ref, 0, 1)
    convolve(ends_ref, 5, params, False, bias, conv_ref, 7, 8, 18)


def tap(kernel, row_tap, col_tap):
    ref, block = kernel
    return ref[row_tap * TAPS + col_tap, block : block + 1, :]


def convolve(source_ref, first_col, kernel_ref, flipped, start, out_ref, first=0, last=SIZE // 4, shift=0):
    def group(index, carry):
        totals = [jnp.broadcast_to(start, (SIZE, WIDTH)) for _ in range(4)]
        for col_tap in range(TAPS):
            for row in range(4 + TAPS - 1):
                values = source_ref[index * 4 + row - shift, first_col + col_tap : first_col + col_tap + SIZE, :]
                for out in range(max(0, row - TAPS + 1), min(4, row + 1)):
                    a, e = row - out, col_tap
                    if flipped:
                        a, e = TAPS - 1 - a, TAPS - 1 - e
                    totals[out] = totals[out] + values * tap(kernel_ref, a, e)
        for out in range(4):
            out_ref[pl.ds(pl.multiple_of(index * 128 + out * SIZE, SIZE), SIZE), :] = totals[out]
        return carry

    lax.fori_loop(first, last, group, 0, unroll=2 if last - first > 1 else True)


def kernel_sums(padded_ref, grad_ref, sums_ref):
    sums_ref[...] = jnp.zeros_like(sums_ref)

    def group(index, carry):
        grads = [
            grad_ref[pl.ds(pl.multiple_of(index * 128 + row * SIZE, SIZE), SIZE), :] for row in range(4)
        ]
        for col_tap in range(TAPS):
            totals = [jnp.zeros((8, WIDTH), F32) for _ in range(TAPS)]
            for row in range(4 + TAPS - 1):
                values = padded_ref[index * 4 + row, 5 + col_tap : 5 + col_tap + SIZE, :]
                for out in range(max(0, row - TAPS + 1), min(4, row + 1)):
                    product = values * grads[out]
                    totals[row - out] = totals[row - out] + (
                        (product[0:8] + product[8:16]) + (product[16:24] + product[24:32])
                    )
            for row_tap in range(TAPS):
                at = 8 * (row_tap * TAPS + col_tap)
                sums_ref[at : at + 8, :] += totals[row_tap]
        return carry

    lax.fori_loop(0, SIZE // 4, group, 0, unroll=2)


def row_rim(grown_ref, kernel_ref, top):
    rows = []
    for depth in range(3):
        total = jnp.zeros((PAD_COLS, WIDTH), F32)
        for row_tap in range(TAPS):
            source = depth - row_tap if top else 35 + depth - row_tap
            if 0 <= source < SIZE:
                for col_tap in range(TAPS):
                    at = 11 - col_tap
                    total = total + grown_ref[source + 3, at : at + PAD_COLS, :] * tap(kernel_ref, row_tap, col_tap)
        rows.append(total)
    return jnp.concatenate(rows, axis=0)


def col_rim(grown_ref, kernel_ref, left, out_ref):
    def group(index, carry):
        totals = [jnp.zeros((8, WIDTH), F32) for _ in range(8)]
        for col_tap in range(3) if left else range(4, TAPS):
            at = 11 - col_tap if left else 51 - col_tap
            for row in range(8 + TAPS - 1):
                values = grown_ref[index * 8 + row, at : at + 8, :]
                for out in range(max(0, row - TAPS + 1), min(8, row + 1)):
                    totals[out] = totals[out] + values * tap(kernel_ref, TAPS - 1 - (row - out), col_tap)
        for out in range(8):
            out_ref[pl.ds(pl.multiple_of(index * 64 + out * 8, 8), 8), :] = totals[out]
        return carry

    lax.fori_loop(0, SIZE // 8, group, 0, unroll=True)


def send_rims(here, grown_ref, kernel, rim_ref, sent_ref):
    rows = (MESSAGE, 3 * PAD_COLS)
    place = onehot(row_rim_slots(iota(rows, 1), True) == iota(rows, 0))
    rims = []
    for facing in range(2):
        rim = row_rim(grown_ref, kernel, facing == 0).astype(BF)
        sent_ref[(1 - side_of(here, 2), side_of(here, 2))[facing]] = matmul(place, rim).astype(BF)
        rims.append(rim)
    cols = (MESSAGE, SIZE * 8)
    for left in (True, False):
        col_rim(grown_ref, kernel, left, rim_ref)
        place = onehot(col_rim_slots(iota(cols, 1), 5 if left else 0) == iota(cols, 0))
        message = matmul(place, rim_ref[...].astype(BF))
        flip = side_of(here - 1 if left else here + 1, 2)
        for rim, base in ((rims[0], 112 - 16 * flip), (rims[1], 96 + 16 * flip)):
            slots = row_rim_slots(iota(rows, 1), False, base if left else None, None if left else base)
            message = message + matmul(onehot(slots == iota(rows, 0)), rim)
        side = side_of(here, 0)
        sent_ref[3 - side if left else 2 + side] = message.astype(BF)


def normalised(conv):
    centred = conv - jnp.mean(conv, axis=1, keepdims=True)
    inv_std = lax.rsqrt(jnp.mean(centred * centred, axis=1, keepdims=True) + EPSILON)
    return centred * inv_std, inv_std


def forward_chunk(conv, field, rows, up_w, up_b, down_w):
    gain, offset, down_b, scale = rows
    standard, _ = normalised(conv)
    normed = (standard * gain + offset).astype(BF)
    pre = matmul(normed, up_w) + up_b
    tangent = jnp.tanh(pre * (GELU_C + (GELU_C * GELU_A) * pre * pre))
    activated = (0.5 * pre * (1.0 + tangent)).astype(BF)
    branch = matmul(activated, down_w) + down_b
    return (field.astype(F32) + scale * branch).astype(BF)


def block_rows(params_ref, block):
    rows = [params_ref[row, block : block + 1, :] for row in range(TAPS * TAPS, PARAM_ROWS)]
    return (*rows[:5], jnp.concatenate(rows[5:], axis=1))


EDGE = 4 * SIZE
INSIDE = CELLS - 2 * EDGE


def first_inside_kernel(
    here_ref, field_ref, a_ref, b_ref, params_ref, up_ref, down_ref,
    out_ref, conv_ref, inside_ref, full_ref,
):
    fill_inside(inside_ref, here_ref[0], field_ref[...], a_ref[...], b_ref[...])
    bias, gain, offset, down_b, scale, up_b = block_rows(params_ref, 0)
    convolve(inside_ref, 5, (params_ref, 0), False, bias, full_ref, 1, 7, 3)

    def chunk(index, carry):
        at = pl.ds(pl.multiple_of(index * CHUNK, CHUNK), CHUNK)
        cells = pl.ds(pl.multiple_of(EDGE + index * CHUNK, EDGE), CHUNK)
        conv = full_ref[cells, :]
        conv_ref[at, :] = conv
        out_ref[at, :] = forward_chunk(
            conv, field_ref[cells, :], (gain, offset, down_b, scale), up_ref[0], up_b, down_ref[0]
        )
        return carry

    lax.fori_loop(0, INSIDE // CHUNK, chunk, 0, unroll=True)


def ends(ref):
    return jnp.concatenate([ref[:EDGE, :], ref[CELLS - EDGE :, :]], axis=0)


def join_rows(ref, inside, edges):
    ref[:EDGE, :] = edges[:EDGE]
    ref[EDGE : CELLS - EDGE, :] = inside
    ref[CELLS - EDGE :, :] = edges[EDGE:]


def first_kernel(
    here_ref, field_ref, c_ref, d_ref, inside_ref, out_in_ref, gather_ref, params_ref, up_ref, down_ref,
    out_ref, conv_ref, rims_ref, sent_ref, ends_ref, full_ref,
):
    here = here_ref[0]
    fill_ends(ends_ref, rims_ref, here, inside_ref, c_ref[...], d_ref[...])
    bias, gain, offset, down_b, scale, up_b = block_rows(params_ref, 0)
    convolve_ends(ends_ref, (params_ref, 0), bias, full_ref)
    conv = ends(full_ref)
    conv_ref[...] = conv
    out = forward_chunk(conv, ends(field_ref), (gain, offset, down_b, scale), up_ref[0], up_b, down_ref[0])
    join_rows(out_ref, out_in_ref[...], out)
    send_cells(here, gather_ref[...], out_ref[...], sent_ref)


def again(block, conv, refs):
    params_ref, up_ref, down_ref = refs
    _, gain, offset, down_b, _, up_b = block_rows(params_ref, block)
    standard, inv_std = normalised(conv)
    normed = (standard * gain + offset).astype(BF)
    pre = matmul(normed, up_ref[block]) + up_b
    square = pre * pre
    tangent = jnp.tanh(pre * (GELU_C + (GELU_C * GELU_A) * square))
    half = 0.5 + 0.5 * tangent
    activated = (pre * half).astype(BF)
    slope = half + pre * (0.5 - 0.5 * tangent * tangent) * (GELU_C + (3.0 * GELU_C * GELU_A) * square)
    branch = matmul(activated, down_ref[block]) + down_b
    return standard, inv_std, normed, activated, slope, branch


def backward_chunk(block, saved, upstream, refs):
    params_ref, up_ref, down_ref, up_sum, down_sum, vector_sum, up_b_sum = refs
    standard, inv_std, normed, activated, slope, branch = saved
    _, gain, _, _, scale, _ = block_rows(params_ref, block)
    scaled = upstream * scale
    scaled_b = scaled.astype(BF)
    down_sum[...] += matmul(scaled_b, activated, ((0,), (0,)))
    pre_grad = matmul(scaled_b, down_ref[block], ((1,), (1,))) * slope
    up_b_sum[...] += jnp.sum(pre_grad, axis=0, keepdims=True)
    pre_grad_b = pre_grad.astype(BF)
    up_sum[...] += matmul(normed, pre_grad_b, ((0,), (0,)))
    normed_grad = matmul(pre_grad_b, up_ref[block], ((1,), (1,)))
    std_grad = normed_grad * gain
    conv_grad = inv_std * (
        std_grad
        - jnp.mean(std_grad, axis=1, keepdims=True)
        - standard * jnp.mean(std_grad * standard, axis=1, keepdims=True)
    )
    for row, values in enumerate((conv_grad, normed_grad * standard, normed_grad, scaled, upstream * branch)):
        vector_sum[row : row + 1, :] += jnp.sum(values, axis=0, keepdims=True)
    return conv_grad


def through(block, conv, upstream, field, refs):
    saved = again(block, conv, refs[:3])
    scale = block_rows(refs[0], block)[4]
    out = (field.astype(F32) + scale * saved[5]).astype(BF)
    return backward_chunk(block, saved, upstream, refs), out


def clear(refs):
    for ref in refs:
        ref[...] = jnp.zeros_like(ref)


def fill_grown(grown_ref, grad):
    grown_ref[0:3] = jnp.zeros((3, GROWN_COLS, WIDTH), F32)
    grown_ref[35:38] = jnp.zeros((3, GROWN_COLS, WIDTH), F32)
    grown_ref[3:35, 0:16] = jnp.zeros((SIZE, 16, WIDTH), F32)
    grown_ref[3:35, 48:64] = jnp.zeros((SIZE, 16, WIDTH), F32)
    grown_ref[3:35, 16:48] = grad.reshape(SIZE, SIZE, WIDTH)


def pack_sums(refs, weights_ref, vectors_ref):
    up_sum, down_sum, vector_sum, up_b_sum = refs[3:]
    for part in range(HID // WIDTH):
        lanes = slice(part * WIDTH, (part + 1) * WIDTH)
        weights_ref[part * WIDTH : (part + 1) * WIDTH, :] = up_sum[:, lanes].astype(BF)
        weights_ref[HID + part * WIDTH : HID + (part + 1) * WIDTH, :] = down_sum[:, lanes].astype(BF)
        vector_sum[8 + part : 9 + part, :] = up_b_sum[:, lanes]
    vectors_ref[...] = vector_sum[...].astype(BF)


def second_inside_kernel(
    here_ref, field_ref, a_ref, b_ref, cotangent_ref, params_ref, up_ref, down_ref,
    out_ref, inside_ref, grad_ref, up_sum, down_sum, vector_sum, up_b_sum, conv_ref,
):
    fill_inside(inside_ref, here_ref[0], field_ref[...], a_ref[...], b_ref[...])
    convolve(inside_ref, 5, (params_ref, 1), False, block_rows(params_ref, 1)[0], conv_ref, 1, 7, 3)
    refs = (params_ref, up_ref, down_ref, up_sum, down_sum, vector_sum, up_b_sum)
    clear(refs[3:])

    def chunk(index, carry):
        at = pl.ds(pl.multiple_of(index * CHUNK, CHUNK), CHUNK)
        cells = pl.ds(pl.multiple_of(EDGE + index * CHUNK, EDGE), CHUNK)
        grad_ref[at, :], out_ref[at, :] = through(
            1, conv_ref[cells, :], cotangent_ref[cells, :].astype(F32), field_ref[cells, :], refs
        )
        return carry

    lax.fori_loop(0, INSIDE // CHUNK, chunk, 0, unroll=True)


def second_kernel(
    here_ref, field_ref, c_ref, d_ref, inside_ref, grad_in_ref, up_in, down_in, vector_in, up_b_in,
    cotangent_ref, params_ref, up_ref, down_ref,
    out_ref, rims_ref, grad_ref, sent_ref, weights_ref, sums_ref,
    ends_ref, conv_ref, grown_ref, up_sum, down_sum, vector_sum, up_b_sum, rim_ref,
):
    here = here_ref[0]
    fill_ends(ends_ref, rims_ref, here, inside_ref, c_ref[...], d_ref[...])
    convolve_ends(ends_ref, (params_ref, 1), block_rows(params_ref, 1)[0], conv_ref)
    refs = (params_ref, up_ref, down_ref, up_sum, down_sum, vector_sum, up_b_sum)
    for ref, start in zip(refs[3:], (up_in, down_in, vector_in, up_b_in)):
        ref[...] = start[...]
    grad, out_ref[...] = through(1, ends(conv_ref), ends(cotangent_ref).astype(F32), ends(field_ref), refs)
    join_rows(grad_ref, grad_in_ref[...], grad)
    fill_grown(grown_ref, grad_ref[...])
    send_rims(here, grown_ref, (params_ref, 1), rim_ref, sent_ref)
    pack_sums(refs, weights_ref, sums_ref)


def third_again_kernel(
    conv_ref, conv_edge_ref, params_ref, up_ref, down_ref,
    standard_ref, inv_std_ref, normed_ref, activated_ref, slope_ref, branch_ref, full_ref,
):
    join_rows(full_ref, conv_ref[...], conv_edge_ref[...])

    def chunk(index, carry):
        at = pl.ds(pl.multiple_of(index * CHUNK, CHUNK), CHUNK)
        saved = again(0, full_ref[at, :], (params_ref, up_ref, down_ref))
        standard_ref[at, :], _, normed_ref[at, :], activated_ref[at, :], slope_ref[at, :], branch_ref[at, :] = saved
        inv_std_ref[at, :] = jnp.broadcast_to(saved[1], (CHUNK, WIDTH))
        return carry

    lax.fori_loop(0, CELLS // CHUNK, chunk, 0, unroll=True)


def third_kernel(
    here_ref, standard_ref, inv_std_ref, normed_ref, activated_ref, slope_ref, branch_ref, base_ref, c_ref, d_ref,
    scatter_ref, params_ref, up_ref, down_ref,
    upstream_ref, grad_ref, sent_ref, weights_ref, sums_ref,
    grown_ref, up_sum, down_sum, vector_sum, up_b_sum, rim_ref,
):
    upstream_ref[...] = base_ref[...] + owned(scatter_ref, 0, c_ref, d_ref)
    refs = (params_ref, up_ref, down_ref, up_sum, down_sum, vector_sum, up_b_sum)
    clear(refs[3:])
    saved_refs = (standard_ref, inv_std_ref, normed_ref, activated_ref, slope_ref, branch_ref)

    def chunk(index, carry):
        at = pl.ds(pl.multiple_of(index * CHUNK, CHUNK), CHUNK)
        grad_ref[at, :] = backward_chunk(0, [ref[at, :] for ref in saved_refs], upstream_ref[at, :], refs)
        return carry

    lax.fori_loop(0, CELLS // CHUNK, chunk, 0, unroll=True)
    fill_grown(grown_ref, grad_ref[...])
    send_rims(here_ref[0], grown_ref, (params_ref, 0), rim_ref, sent_ref)
    pack_sums(refs, weights_ref, sums_ref)


def owned(scatter_ref, first, *refs):
    lanes = slice(first * MESSAGE, (first + len(refs)) * MESSAGE)
    return matmul(scatter_ref[:, lanes], jnp.concatenate([ref[...] for ref in refs], axis=0))


def last_kernel(base_ref, c_ref, d_ref, scatter_ref, out_ref):
    out_ref[...] = (base_ref[...] + owned(scatter_ref, 0, c_ref, d_ref)).astype(BF)


def make_inner_kernel(block):
    def inner_kernel(grad_ref, upstream_ref, a_ref, b_ref, scatter_ref, params_ref, base_ref, grown_ref):
        fill_grown(grown_ref, grad_ref[...])
        convolve(grown_ref, 13, (params_ref, block), True, jnp.zeros((1, WIDTH), F32), base_ref)
        base_ref[...] += upstream_ref[...].astype(F32) + owned(scatter_ref, 2, a_ref, b_ref)

    return inner_kernel


def fill_padded(padded_ref, inside_ref, rims_ref):
    padded_ref[0:3] = rims_ref[0:3]
    padded_ref[3:35] = inside_ref[...]
    padded_ref[35:38] = rims_ref[3:6]


def taps_and_out_kernel(
    pad_inside_ref, pad_rims_ref, grad_ref, inside_ref, edges_ref, taps_ref, out_ref, padded_ref, sums_ref
):
    join_rows(out_ref, inside_ref[...], edges_ref[...])
    fill_padded(padded_ref, pad_inside_ref, pad_rims_ref)
    taps_kernel(padded_ref, grad_ref, taps_ref, sums_ref)


def taps_kernel(padded_ref, grad_ref, taps_ref, sums_ref):
    kernel_sums(padded_ref, grad_ref, sums_ref)
    taps_ref[...] = jnp.sum(sums_ref[...].reshape(64, 8, WIDTH), axis=1).astype(BF)


def halves_kernel(
    core_ref, pad_inside_ref, pad_rims_ref, grad_ref, weights_0_ref, sums_0_ref, weights_1_ref, sums_1_ref, taps_1_ref,
    kept_ref, given_ref, taps_ref, padded_ref, partial_ref,
):
    fill_padded(padded_ref, pad_inside_ref, pad_rims_ref)
    taps_kernel(padded_ref, grad_ref, taps_ref, partial_ref)

    def fill(half_ref, *parts):
        at = 0
        for part in parts:
            half_ref[at : at + part.shape[0], :] = part[...]
            at += part.shape[0]
        half_ref[at:, :] = jnp.zeros((HALF_ROWS - at, WIDTH), BF)

    first = (weights_0_ref, sums_0_ref, taps_ref)
    second = (weights_1_ref, sums_1_ref, taps_1_ref)
    for core, kept, given in ((0, first, second), (1, second, first)):

        @pl.when(core_ref[0] == core)
        def _(kept=kept, given=given):
            fill(kept_ref, *kept)
            fill(given_ref, *given)


def swapped_tiles(value, step, odd):
    starts = [tile for tile in range(TILES) if (tile // step) % 2 == odd]
    pairs = [(tile, (tile + step) % TILES) for tile in starts]
    return lax.ppermute(value, TILE_AXES, pairs + [(target, source) for source, target in pairs])


def beside(sent):
    by_b = swapped_tiles(sent[3], 1, 1)
    return swapped_tiles(sent[2], 1, 0), by_b


def beyond(sent, by_a, by_b):
    by_c = swapped_tiles(jnp.concatenate([sent[0, :96], by_a[96:112], by_b[96:112]]), 4, 0)
    by_d = swapped_tiles(jnp.concatenate([sent[1, :96], by_a[112:], by_b[112:]]), 4, 1)
    return by_c, by_d


HALF_ROWS = 1152


def swapped(value, axis):
    return lax.ppermute(value, axis, [(0, 1), (1, 0)])


def summed_apart(value, axes):
    count = lax.axis_size(axes)
    parts = lax.all_to_all(value, axes, 0, 0, tiled=True).reshape(count, -1, WIDTH)
    return jnp.sum(parts.astype(F32), axis=0).astype(BF)


def gathered(value, axes):
    count = lax.axis_size(axes)
    copies = jnp.broadcast_to(value[None], (count,) + value.shape).reshape(-1, WIDTH)
    return lax.all_to_all(copies, axes, 0, 0, tiled=True)


ACROSS = ("far", "y", "member")


def summed_along(value, axis):
    count = lax.axis_size(axis)
    return jnp.sum(gathered(value, axis).reshape(count, -1, WIDTH).astype(F32), axis=0).astype(BF)


def make_unpack_kernel(factor):
    def unpack_kernel(core_ref, mine_ref, other_ref, taps, conv_b, gain, offset, up, up_b, down, down_b, scale):
        def unpack(sum_ref, block):
            for part in range(HID // WIDTH):
                rows = slice(part * WIDTH, (part + 1) * WIDTH)
                up[block, :, part * WIDTH : (part + 1) * WIDTH] = sum_ref[rows, :].astype(F32) * factor
                rows = slice(HID + part * WIDTH, HID + (part + 1) * WIDTH)
                down[block, part * WIDTH : (part + 1) * WIDTH, :] = (sum_ref[rows, :].astype(F32) * factor).T
            base = 2 * HID
            vectors = sum_ref[base : base + 16, :].astype(F32) * factor
            for row, ref in enumerate((conv_b, gain, offset, down_b, scale)):
                ref[block : block + 1, :] = vectors[row : row + 1]
            for part in range(HID // WIDTH):
                up_b[block : block + 1, part * WIDTH : (part + 1) * WIDTH] = vectors[8 + part : 9 + part]
            base += 16
            kernel_sum = sum_ref[base : base + 64, :].astype(F32) * factor
            for row in range(TAPS * TAPS):
                taps[row, block : block + 1, :] = kernel_sum[row : row + 1]

        for core in range(2):

            @pl.when(core_ref[0] == core)
            def _(core=core):
                unpack(mine_ref, core)
                unpack(other_ref, 1 - core)

    return unpack_kernel


def laid_down(items):
    rows = sum(item.shape[0] for item in items)
    total, at = None, 0
    for item in items:
        edges = [(at, rows - at - item.shape[0], 0)] + [(0, 0, 0)] * (item.ndim - 1)
        part = lax.pad(item, jnp.zeros((), item.dtype), edges)
        total = part if total is None else total + part
        at += item.shape[0]
    return total


def shaped(*shapes):
    return [jax.ShapeDtypeStruct(shape, dtype) for shape, dtype in shapes]


def call(kernel, shapes, inputs, scratch=(), scalars=0, cost=None):
    specs = [pl.BlockSpec(memory_space=pltpu.SMEM)] * scalars + whole(len(inputs) - scalars)
    return pl.pallas_call(
        kernel,
        out_shape=shaped(*shapes),
        in_specs=specs,
        out_specs=whole(len(shapes)),
        scratch_shapes=list(scratch),
        compiler_params=kernel_params(),
        cost_estimate=cost,
    )(*inputs)


def body(
    states, cotangent, seam_codes, corner_codes, dw_kernel, dw_bias, norm_gain, norm_bias, up_weight, up_bias,
    down_weight, down_bias, layer_scale,
):
    count = lax.axis_size(TILE_AXES) * lax.axis_size("member")
    here = lax.axis_index(TILE_AXES).astype(jnp.int32).reshape(1)
    field = states.reshape(CELLS, WIDTH)
    upstream = cotangent.reshape(CELLS, WIDTH)
    message = ((4, MESSAGE, WIDTH), BF)
    inside_shape = ((SIZE, PAD_COLS, WIDTH), F32)
    rims_shape = ((6, PAD_COLS, WIDTH), F32)
    ends_scratch = pltpu.VMEM((20, PAD_COLS, WIDTH), F32)
    weights_shape = ((2 * HID, WIDTH), BF)
    sums_shape = ((16, WIDTH), BF)
    cells = (CELLS, WIDTH)
    inside, edges = (INSIDE, WIDTH), (2 * EDGE, WIDTH)
    wide_sums = [((WIDTH, HID), F32), ((WIDTH, HID), F32), ((16, WIDTH), F32), ((1, HID), F32)]
    padded_scratch = pltpu.VMEM((PAD_ROWS, PAD_COLS, WIDTH), F32)
    grown_scratch = pltpu.VMEM((PAD_ROWS, GROWN_COLS, WIDTH), F32)
    cells_scratch = pltpu.VMEM(cells, F32)
    sums = [grown_scratch, *(pltpu.VMEM(*item) for item in wide_sums), pltpu.VMEM((SIZE * 8, WIDTH), F32)]
    tap_scratch = [pltpu.VMEM((64 * 8, WIDTH), F32)]
    vpu = pl.CostEstimate(flops=2 * 49 * CELLS * WIDTH, bytes_accessed=3 << 20, transcendentals=0)

    codes = jnp.concatenate([seam_codes.T, corner_codes.T])
    sent, gather, owners = call(
        select_kernel,
        [message, ((4 * MESSAGE, CELLS), BF), ((4, 8, MESSAGE), jnp.int32)],
        [here, codes, field],
        scalars=2,
    )
    near = beside(sent)
    packed = laid_down(
        [dw_kernel.transpose(1, 2, 0, 3).reshape(TAPS * TAPS, BLOCKS, WIDTH)]
        + [item[None] for item in (dw_bias, norm_gain, norm_bias, down_bias, layer_scale)]
        + [up_bias.reshape(BLOCKS, HID // WIDTH, WIDTH).transpose(1, 0, 2)]
    )
    near, packed = lax.optimization_barrier((near, packed))
    params = (packed, up_weight, down_weight)
    far = beyond(sent, *near)
    part, conv_part, pad_inside_0 = call(
        first_inside_kernel,
        [(inside, BF), (inside, F32), inside_shape],
        [here, field, *near, *params],
        [cells_scratch],
        scalars=1,
        cost=vpu,
    )
    middle, conv_edges, pad_rims_0, sent = call(
        first_kernel,
        [(cells, BF), (edges, F32), rims_shape, message],
        [here, field, *far, pad_inside_0, part, gather, *params],
        [ends_scratch, cells_scratch],
        scalars=1,
    )
    near = beside(sent)
    (scatter,) = call(scatter_kernel, [((CELLS, 4 * MESSAGE), BF)], [owners], cost=vpu)
    near, scatter = lax.optimization_barrier((near, scatter))
    far = beyond(sent, *near)
    out_part, pad_inside_1, *partial = call(
        second_inside_kernel,
        [(inside, BF), inside_shape, (inside, F32), *wide_sums],
        [here, middle, *near, upstream, *params],
        [cells_scratch],
        scalars=1,
        cost=vpu,
    )
    out_edges, pad_rims_1, grad_1, sent, weights_1, sums_1 = call(
        second_kernel,
        [(edges, BF), rims_shape, (cells, F32), message, weights_shape, sums_shape],
        [here, middle, *far, pad_inside_1, *partial, upstream, *params],
        [ends_scratch, cells_scratch, *sums],
        scalars=1,
    )
    near = beside(sent)
    taps_1, out = call(
        taps_and_out_kernel,
        [((64, WIDTH), BF), (cells, BF)],
        [pad_inside_1, pad_rims_1, grad_1, out_part, out_edges],
        [padded_scratch, *tap_scratch],
        cost=vpu,
    )
    near, taps_1 = lax.optimization_barrier((near, taps_1))
    far = beyond(sent, *near)
    (base_1,) = call(
        make_inner_kernel(1),
        [(cells, F32)],
        [grad_1, upstream, *near, scatter, packed],
        [grown_scratch],
        cost=vpu,
    )
    saved = call(
        third_again_kernel,
        [(cells, F32), (cells, F32), (cells, BF), ((CELLS, HID), BF), ((CELLS, HID), F32), (cells, F32)],
        [conv_part, conv_edges, *params],
        [cells_scratch],
        cost=vpu,
    )
    far, base_1, saved = lax.optimization_barrier((far, base_1, saved))
    upstream_0, grad_0, sent, weights_0, sums_0 = call(
        third_kernel,
        [(cells, F32), (cells, F32), message, weights_shape, sums_shape],
        [here, *saved, base_1, *far, scatter, *params],
        sums,
        scalars=1,
    )
    near = beside(sent)
    core = lax.axis_index("core").astype(jnp.int32).reshape(1)
    kept, given = call(
        halves_kernel,
        [((HALF_ROWS, WIDTH), BF), ((HALF_ROWS, WIDTH), BF)],
        [core, pad_inside_0, pad_rims_0, grad_0, weights_0, sums_0, weights_1, sums_1, taps_1],
        [pltpu.VMEM((64, WIDTH), BF), padded_scratch, *tap_scratch],
        scalars=1,
    )
    total = (kept.astype(F32) + swapped(given, "core").astype(F32)).astype(BF)
    total = summed_apart(total, ACROSS)
    total, near = lax.optimization_barrier((total, near))
    far = beyond(sent, *near)
    (base_0,) = call(
        make_inner_kernel(0),
        [(cells, F32)],
        [grad_0, upstream_0, *near, scatter, packed],
        [grown_scratch],
        cost=vpu,
    )
    total = summed_along(total, "z")
    (by_c, by_d), (total, by_c) = far, lax.optimization_barrier((total, far[0]))
    far = (by_c, by_d)
    total = gathered(total, ACROSS)
    total, far, base_0 = lax.optimization_barrier((total, far, base_0))
    (grad_field,) = call(last_kernel, [(cells, BF)], [base_0, *far, scatter])
    halves = (total, swapped(total, "core"))
    row, wide = ((BLOCKS, WIDTH), F32), ((BLOCKS, HID), F32)
    grads = call(
        make_unpack_kernel(1.0 / math.sqrt(count * CELLS)),
        [
            ((TAPS * TAPS, BLOCKS, WIDTH), F32), row, row, row, ((BLOCKS, WIDTH, HID), F32), wide,
            ((BLOCKS, HID, WIDTH), F32), row, row,
        ],
        [core, *halves],
        scalars=1,
    )
    kernel_grad = grads[0].reshape(TAPS, TAPS, BLOCKS, WIDTH).transpose(2, 0, 1, 3)
    shape = states.shape
    return (out.reshape(shape), grad_field.reshape(shape), kernel_grad, *grads[1:])


def solution(mesh):
    split = Mesh(mesh.devices.reshape(2, 4, 8, 2, 2), (*TILE_AXES, "member"))
    field = P("member", TILE_AXES, None, None, None)
    return jax.shard_map(
        body,
        mesh=split,
        in_specs=(field, field) + (P(),) * 11,
        out_specs=(field, field) + (P(),) * 9,
        check_vma=False,
    )
```
